32 devices in a mesh: lat: 8 (over z, core), lon: 4 (over y, x).
Axes of the slice: x: 2, y: 2, z: 4, core: 2. Of those that a mesh axis runs over, the one named last changes fastest.
Arguments:
- ensemble: float32 [3, 80, 256, 512], P(None, None, 'lat', 'lon'), may hold values from -6 to 6
- courant_cols: float32 [1, 256, 512], P(None, 'lat', 'lon'), may hold values from -0.6 to 0.6
- courant_rows: float32 [1, 256, 512], P(None, 'lat', 'lon'), may hold values from -0.6 to 0.6
- obs_value: float32 [2, 768], P(None, ('lat', 'lon')), may hold values from -8 to 8
- obs_error: float32 [2, 768], P(None, ('lat', 'lon')), may hold values from 0.2 to 2
- obs_cell: int32 [2, 768], P(None, ('lat', 'lon')), may hold values from 0 to 4095
- obs_kind: int32 [2, 768], P(None, ('lat', 'lon')), may hold values from 0 to 2
- obs_live: int32 [2, 768], P(None, ('lat', 'lon')), may hold values from 0 to 1, as said below
- obs_list: int32 [2, 768, 9], P(None, ('lat', 'lon')), may hold values 0 or 1
Outputs:
- analysis: float32 [3, 80, 256, 512], P(None, None, 'lat', 'lon')
The draws below stay inside these ranges and needn't reach their ends.
Inputs may be any that keep to these rules, and one draw needn't show every extreme that they name: `obs_live`: in each batch the live slots of a tile are its first ones, and in every batch some tile has all 24 slots live.
All inputs are finite; a program needn't handle non-finite values. No bound on the sum of `obs_list` on one device may be relied on, other than what follows from the above.
Results may differ from the reference program's by a relative error of at most 0.0003.
Values sent between devices are 32-bit elements; how exact they have to be, the bound alone decides.
A program may use at most 64 MiB of HBM per device.

```python
import math
import jax
import jax.numpy as jnp
from jax import lax

MEMBERS = 80
LEVELS = 1
FIELD_LEVELS = 3
TILE_ROWS = 32
TILE_COLS = 128
OBS_TILE = 24
GRID_ROWS = 256
GRID_COLS = 512
OBS_SLOTS = 768
N_LAT = 8
N_LON = 4


def draw_obs_live(key, part):
    first, second, third = jax.random.split(key, 3)
    tiles = OBS_SLOTS // OBS_TILE
    count_a = jax.random.randint(first, (2, tiles), 1, OBS_TILE + 1)
    count_b = jax.random.randint(second, (2, tiles), 1, OBS_TILE + 1)
    counts = jnp.maximum(count_a, count_b)
    fullest = jax.random.randint(third, (2,), 0, tiles)
    counts = jnp.where(jnp.arange(tiles)[None, :] == fullest[:, None], OBS_TILE, counts)
    live = (jnp.arange(OBS_TILE)[None, None, :] < counts[:, :, None]).astype(jnp.int32)
    return live.reshape(2, OBS_SLOTS)


def plant(values, rng, low, largest):
    extent = values.shape
    index_at = [jax.random.randint(jax.random.fold_in(rng, axis), (), 0, extent[axis]) for axis in range(len(extent))]
    values = values.at[tuple(index_at)].set(low)
    longest = extent.index(max(extent))
    index_at[longest] = (index_at[longest] + 1) % extent[longest]
    return values.at[tuple(index_at)].set(largest)


def levels(rng, shape, shards, least, high):
    level = 1.0
    for dim, shards_of in shards:
        steps = jax.random.uniform(jax.random.fold_in(jax.random.fold_in(rng, 6), dim), (shards_of,), jnp.float32, least / len(shards), high / len(shards))
        level = level * jnp.repeat(jnp.exp(steps), shape[dim] // shards_of).reshape((-1,) + (1,) * (len(shape) - 1 - dim))
    return level


def normal_values(own_key, extent, scale, bound, cuts=(), kind=jnp.bfloat16):
    factor_of = levels(own_key, extent, cuts, -0.22, 0.18) if cuts else 1.0
    values = jax.random.normal(own_key, extent, jnp.float32) * scale * factor_of
    return jnp.minimum(jnp.maximum(values, -bound), bound).astype(kind)


def setup_inputs(seed: int = 0) -> dict:
    key_of = jax.random.split(jax.random.key(seed), 10)
    ensemble = normal_values(key_of[0], (FIELD_LEVELS, MEMBERS, GRID_ROWS, GRID_COLS), 1.0, 6.0, ((2, 8), (3, 4)), jnp.float32)
    courant_cols = jnp.clip(jax.random.uniform(key_of[1], (LEVELS, GRID_ROWS, GRID_COLS), jnp.float32, -0.6, 0.6) * levels(key_of[1], (LEVELS, GRID_ROWS, GRID_COLS), ((1, 8), (2, 4)), -0.4, 0.0), -0.6, 0.6)
    courant_rows = jnp.clip(jax.random.uniform(key_of[2], (LEVELS, GRID_ROWS, GRID_COLS), jnp.float32, -0.6, 0.6) * levels(key_of[2], (LEVELS, GRID_ROWS, GRID_COLS), ((1, 8), (2, 4)), -0.4, 0.0), -0.6, 0.6)
    obs_value = normal_values(key_of[3], (2, OBS_SLOTS), 1.5, 8.0, ((1, 32),), jnp.float32)
    obs_error = jnp.clip(jnp.exp(math.log(2.0) - 2.3025851 * jax.random.uniform(key_of[4], (2, OBS_SLOTS), jnp.float32) ** levels(key_of[4], (2, OBS_SLOTS), ((1, 32),), -0.2, 0.2)), 0.2, 2.0)
    obs_cell = plant(jax.random.randint(key_of[5], (2, OBS_SLOTS), 0, TILE_ROWS * TILE_COLS), jax.random.fold_in(key_of[5], 1), 0, (TILE_ROWS * TILE_COLS) - 1).astype(jnp.int32)
    obs_kind = plant(jax.random.randint(key_of[6], (2, OBS_SLOTS), 0, FIELD_LEVELS), jax.random.fold_in(key_of[6], 1), 0, FIELD_LEVELS - 1).astype(jnp.int32)
    obs_live = draw_obs_live(jax.random.fold_in(key_of[9], 71), 0)
    obs_list = plant((jax.random.randint(key_of[8], (2, OBS_SLOTS, 9), 0, 4) < 3).astype(jnp.int32), jax.random.fold_in(key_of[8], 1), 0, 1)
    return {"ensemble": ensemble, "courant_cols": courant_cols, "courant_rows": courant_rows, "obs_value": obs_value, "obs_error": obs_error, "obs_cell": obs_cell, "obs_kind": obs_kind, "obs_live": obs_live, "obs_list": obs_list}


def taper(dist):
    return jnp.square(jnp.maximum(0.0, 1.0 - jnp.abs(dist)))

def advect(state, courant_cols, courant_rows):
    speed_c = jnp.tile(courant_cols, (3, 1, 1))[:, None]
    speed_r = jnp.tile(courant_rows, (3, 1, 1))[:, None]
    padded = jnp.pad(state, ((0, 0), (0, 0), (1, 1), (1, 1)))
    north = padded[:, :, 2:, 1:-1]
    south = padded[:, :, :-2, 1:-1]
    east = padded[:, :, 1:-1, 2:]
    west = padded[:, :, 1:-1, :-2]
    result = state - 0.5 * speed_c * (east - west) + 0.5 * speed_c * speed_c * (east - 2.0 * state + west)
    result = result - 0.5 * speed_r * (north - south) + 0.5 * speed_r * speed_r * (north - 2.0 * state + south)
    return result

def make_table(prior, value, error, live, row_local, col_local, listed):
    members = prior.shape[1]
    ybar = lax.optimization_barrier(jnp.mean(prior, axis=1))
    yperts = prior - ybar[:, None]
    spread = lax.optimization_barrier(jnp.sum(yperts * yperts, axis=1)) / (members - 1)
    total = spread + error
    gain = live.astype(jnp.float32) / total
    alpha = 1.0 / (1.0 + jnp.sqrt(error / total))
    innov = value - ybar
    extra = jnp.stack([gain, innov, alpha, row_local.astype(jnp.float32), col_local.astype(jnp.float32)], axis=1)
    return jnp.concatenate([yperts, extra, listed.astype(jnp.float32)], axis=1)

def assimilate(block, nearby):
    fields, members, trows, tcols = block.shape
    capacity = nearby.shape[2]
    radius = float(trows)
    mean = lax.optimization_barrier(jnp.mean(block, axis=1))
    perts = block - mean[:, None]
    yperts = nearby[:, :, :, :members]
    gain = nearby[:, :, :, members]
    innov = nearby[:, :, :, members + 1]
    alpha = nearby[:, :, :, members + 2]
    orow = nearby[:, :, :, members + 3]
    ocol = nearby[:, :, :, members + 4]
    listed = nearby[:, :, :, members + 5:members + 14]
    offset = jnp.arange(3, dtype=jnp.int32)
    offset_f = offset.astype(jnp.float32) - 1.0
    rows_rel = offset_f[:, None, None] * trows + orow
    cols_rel = offset_f[None, :, None] * tcols + ocol
    slot_of = (2 - offset)[:, None] * 3 + (2 - offset)[None, :]
    onehot = (jnp.arange(9, dtype=jnp.int32)[None, None, :] == slot_of[:, :, None]).astype(jnp.float32)
    chosen = lax.optimization_barrier(jnp.sum(listed * onehot[:, :, None, :], axis=3))
    factor = gain * chosen
    lat_w = taper((rows_rel[..., None] - jnp.arange(trows, dtype=jnp.float32)) / radius) * factor[..., None]
    lon_w = taper((cols_rel[..., None] - jnp.arange(tcols, dtype=jnp.float32)) / radius)
    count = 9 * capacity
    lat_w = lat_w.reshape(count, trows)
    lon_w = lon_w.reshape(count, tcols)
    yperts = yperts.reshape(count, members)
    innov = innov.reshape(count)
    alpha = alpha.reshape(count)
    hi = lax.Precision.HIGHEST
    proj = jnp.einsum('fmij,km->fkij', perts, yperts, precision=hi) / (members - 1)
    weights = proj * lat_w[None, :, :, None] * lon_w[None, :, None, :]
    mean = mean + jnp.einsum('fkij,k->fij', weights, innov, precision=hi)
    perts = perts - jnp.einsum('fkij,km->fmij', weights, alpha[:, None] * yperts, precision=hi)
    return mean[:, None] + perts

def reference(ensemble, courant_cols, courant_rows, obs_value, obs_error, obs_cell, obs_kind, obs_live, obs_list):
    state = advect(ensemble, courant_cols, courant_rows)
    slots = jnp.arange(OBS_SLOTS, dtype=jnp.int32)
    owner = slots // OBS_TILE
    owner_row = owner // N_LON
    owner_col = owner % N_LON
    zero = jnp.zeros((), jnp.int32)
    for batch in range(2):
        row_local = obs_cell[batch] // TILE_COLS
        col_local = obs_cell[batch] % TILE_COLS
        prior = state[obs_kind[batch], :, owner_row * TILE_ROWS + row_local, owner_col * TILE_COLS + col_local]
        table = make_table(prior, obs_value[batch], obs_error[batch], obs_live[batch], row_local, col_local, obs_list[batch])
        width_t = table.shape[1]
        board = jnp.pad(table.reshape(N_LAT, N_LON, OBS_TILE, width_t), ((1, 1), (1, 1), (0, 0), (0, 0)))
        current = state

        def one_tile(tile):
            tile_r = (tile // N_LON).astype(jnp.int32)
            tile_c = (tile % N_LON).astype(jnp.int32)
            nearby = lax.dynamic_slice(board, (tile_r, tile_c, zero, zero), (3, 3, OBS_TILE, width_t))
            block = lax.dynamic_slice(current, (zero, zero, tile_r * TILE_ROWS, tile_c * TILE_COLS), (FIELD_LEVELS, MEMBERS, TILE_ROWS, TILE_COLS))
            return assimilate(block, nearby)
        tiles = lax.map(one_tile, jnp.arange(N_LAT * N_LON, dtype=jnp.int32))
        tiles = tiles.reshape(N_LAT, N_LON, FIELD_LEVELS, MEMBERS, TILE_ROWS, TILE_COLS)
        state = tiles.transpose(2, 3, 0, 4, 1, 5).reshape(FIELD_LEVELS, MEMBERS, GRID_ROWS, GRID_COLS)
    return state
```

```python
import functools
import jax
import jax.numpy as jnp
from jax import lax
from jax.sharding import PartitionSpec as P
from jax.experimental import pallas as pl
from jax.experimental.pallas import tpu as pltpu

MESH = pl.DeviceIdType.MESH
EXTRA = 16
HIGHEST = lax.Precision.HIGHEST
AROUND = [(a, b) for a in (-1, 0, 1) for b in (-1, 0, 1) if (a, b) != (0, 0)]


def slot_of(a, b):
    return (a + 1) * 3 + b + 1


def taper(dist):
    return jnp.square(jnp.maximum(0.0, 1.0 - jnp.abs(dist)))


def pad_rows(x, rows):
    if rows == x.shape[0]:
        return x
    return jnp.concatenate([x, jnp.zeros((rows - x.shape[0], x.shape[1]), x.dtype)], axis=0)


def table_columns(near, members, trows, tcols):
    rows, cols, factor = [], [], []
    for a in (-1, 0, 1):
        for b in (-1, 0, 1):
            block = near[slot_of(a, b)]
            rows.append(block[:, members + 3 : members + 4] + float(a * trows))
            cols.append(block[:, members + 4 : members + 5] + float(b * tcols))
            took = members + 5 + slot_of(-a, -b)
            factor.append(block[:, members + 1 : members + 2] * block[:, took : took + 1])
    return [jnp.concatenate(part, axis=0) for part in (rows, cols, factor)]


def make_table(prior, info):
    members, lanes = prior.shape
    ybar = jnp.sum(prior, axis=0, keepdims=True) / members
    yp = prior - ybar
    spread = jnp.sum(yp * yp, axis=0, keepdims=True) / (members - 1)
    value, live, error = info[0:1], info[1:2], info[2:3]
    total = spread + error
    gain = live / total
    alpha = 1.0 / (1.0 + jnp.sqrt(error / total))
    innov = value - ybar
    at = lax.broadcasted_iota(jnp.int32, info.shape, 0)
    extra = jnp.where(at == 0, innov, jnp.where(at == 1, gain, jnp.where(at == 2, alpha, info)))
    return jnp.transpose(pad_rows(jnp.concatenate([yp, extra], axis=0), lanes))


def exchange_kernel(
    sizes, x_ref, cu_ref, cv_ref, info_ref, where_ref, state_ref, tables_ref,
    xt, pack, halo, near, row_send, row_recv, col_send, col_recv, tab_send, tab_recv,
):
    fields, members, trows, tcols, slots, n_lat, n_lon = sizes
    lat, lon = lax.axis_index("lat"), lax.axis_index("lon")

    def exists(a, b):
        r, c = lat + a, lon + b
        return (r >= 0) & (r < n_lat) & (c >= 0) & (c < n_lon)

    xt[:, 0] = jnp.zeros((fields, members, tcols), jnp.float32)
    xt[:, trows + 1] = jnp.zeros((fields, members, tcols), jnp.float32)
    halo[...] = jnp.zeros(halo.shape, jnp.float32)
    near[...] = jnp.zeros(near.shape, jnp.float32)

    barrier = pltpu.get_barrier_semaphore()
    for a, b in AROUND:
        @pl.when(exists(a, b))
        def _():
            pl.semaphore_signal(barrier, inc=1, device_id=(lat + a, lon + b), device_id_type=MESH)

    lane = lax.broadcasted_iota(jnp.int32, (members, tcols), 1)

    def turn(i, carry):
        west, east = carry
        for f in range(fields):
            tile = x_ref[pl.ds(f * members * trows + i, members, stride=trows), :]
            xt[f, i + 1] = tile
            at = f * trows + i
            here = lane == at
            west = jnp.where(here, jnp.broadcast_to(tile[:, 0:1], tile.shape), west)
            east = jnp.where(here, jnp.broadcast_to(tile[:, tcols - 1 : tcols], tile.shape), east)
        return west, east

    none = jnp.zeros((members, tcols), jnp.float32)
    west, east = lax.fori_loop(0, trows, turn, (none, none))
    pack[0] = west
    pack[1] = east

    lat_i = jnp.int32(1) * lat
    lat_n = jnp.where(lat_i > 0, 1, 0) + jnp.where(lat_i < n_lat - 1, 1, 0) + 1
    lon_n = jnp.where(lon > 0, 1, 0) + jnp.where(lon < n_lon - 1, 1, 0) + 1
    pl.semaphore_wait(barrier, lat_n * lon_n - 1)

    def row_copy(k):
        return pltpu.make_async_remote_copy(
            src_ref=xt.at[:, 1 if k == 0 else trows],
            dst_ref=xt.at[:, trows + 1 if k == 0 else 0],
            send_sem=row_send.at[k], recv_sem=row_recv.at[k],
            device_id=(lat - 1 if k == 0 else lat + 1, lon), device_id_type=MESH,
        )

    def col_copy(k):
        return pltpu.make_async_remote_copy(
            src_ref=pack.at[k], dst_ref=halo.at[k],
            send_sem=col_send.at[k], recv_sem=col_recv.at[k],
            device_id=(lat, lon - 1 if k == 0 else lon + 1), device_id_type=MESH,
        )

    for k, d in ((0, -1), (1, 1)):
        @pl.when(exists(0, d))
        def _():
            col_copy(k).start()

        @pl.when(exists(d, 0))
        def _():
            row_copy(k).start()

    for k, d in ((0, -1), (1, 1)):
        @pl.when(exists(0, d))
        def _():
            col_copy(k).wait_send()

        @pl.when(exists(d, 0))
        def _():
            row_copy(k).wait_send()

        @pl.when(exists(0, -d))
        def _():
            col_copy(k).wait_recv()

        @pl.when(exists(-d, 0))
        def _():
            row_copy(k).wait_recv()

    def advect(i, carry):
        u = jnp.broadcast_to(cu_ref[pl.ds(i, 1), :], (members, tcols))
        v = jnp.broadcast_to(cv_ref[pl.ds(i, 1), :], (members, tcols))
        hu, hv = 0.5 * u, 0.5 * v
        huu, hvv = hu * u, hv * v
        for f in range(fields):
            mid = xt[f, i + 1]
            south = xt[f, i]
            north = xt[f, i + 2]
            at = f * trows + i
            after = pltpu.roll(halo[0], tcols - 1 - at, 1)
            before = pltpu.roll(halo[1], lax.rem(tcols - at, tcols), 1)
            east = jnp.where(lane == tcols - 1, after, pltpu.roll(mid, tcols - 1, 1))
            west = jnp.where(lane == 0, before, pltpu.roll(mid, 1, 1))
            two = 2.0 * mid
            out = mid - hu * (east - west) + huu * (east - two + west)
            out = out - hv * (north - south) + hvv * (north - two + south)
            state_ref[f * trows + i] = out
        return carry

    lax.fori_loop(0, trows, advect, 0)

    def gather(batch):
        def one(s, prior):
            tile = state_ref[where_ref[batch, 0, s]]
            picked = jnp.where(lane == where_ref[batch, 1, s], tile, 0.0)
            column = jnp.sum(picked, axis=1, keepdims=True)
            return jnp.where(lane == s, jnp.broadcast_to(column, tile.shape), prior)

        return lax.fori_loop(0, slots, one, none)

    def table_copy(batch, a, b):
        return pltpu.make_async_remote_copy(
            src_ref=near.at[batch, slot_of(0, 0)],
            dst_ref=near.at[batch, slot_of(-a, -b)],
            send_sem=tab_send.at[batch, slot_of(a, b)],
            recv_sem=tab_recv.at[batch, slot_of(-a, -b)],
            device_id=(lat + a, lon + b), device_id_type=MESH,
        )

    def send(batch):
        for a, b in AROUND:
            @pl.when(exists(a, b))
            def _():
                table_copy(batch, a, b).start()

    def finish(batch):
        for a, b in AROUND:
            @pl.when(exists(a, b))
            def _():
                table_copy(batch, a, b).wait_send()

            @pl.when(exists(-a, -b))
            def _():
                table_copy(batch, a, b).wait_recv()

    near[0, slot_of(0, 0)] = make_table(gather(0), info_ref[0])[:slots]
    send(0)
    later = gather(1)
    finish(0)

    info = info_ref[1]
    board = [near[0, k] for k in range(9)]
    rows, cols, factor = table_columns(board, members, trows, tcols)
    whole = jnp.concatenate(board, axis=0)
    count = whole.shape[0]
    loc = taper((rows - info[3:4]) / trows) * factor * taper((cols - info[4:5]) / trows)
    mean = jnp.sum(later, axis=0, keepdims=True) / members
    pert = later - mean
    shut = lax.broadcasted_iota(jnp.int32, whole.shape, 1)
    yp = jnp.where(shut < members, whole, 0.0)
    proj = jnp.dot(yp, pad_rows(pert, tcols), precision=HIGHEST, preferred_element_type=jnp.float32)
    weight = proj * loc * (1.0 / (members - 1))
    mean = mean + jnp.sum(weight * whole[:, members : members + 1], axis=0, keepdims=True)
    scaled = whole * whole[:, members + 2 : members + 3]
    full = -(-count // tcols) * tcols
    change = jnp.dot(
        jnp.transpose(pad_rows(scaled, full))[:members], pad_rows(weight, full),
        precision=HIGHEST, preferred_element_type=jnp.float32,
    )
    near[1, slot_of(0, 0)] = make_table(mean + pert - change, info)[:slots]
    send(1)
    finish(1)
    tables_ref[...] = near[...]


def split(x):
    hi = x.astype(jnp.bfloat16)
    return hi, (x - hi.astype(jnp.float32)).astype(jnp.bfloat16)


def update_kernel(sizes, state_ref, tables_ref, out_ref, left, back, rowrel, colw):
    fields, members, trows, tcols, slots, high = sizes
    count = 9 * slots
    depth = left.shape[1]
    wide = left.shape[2]
    tall = back.shape[1] // 2
    step = pl.program_id(0)

    @pl.when(step == 0)
    def _():
        for batch in range(2):
            board = [tables_ref[batch, k] for k in range(9)]
            rows, cols, factor = table_columns(board, members, trows, tcols)
            whole = jnp.concatenate(board, axis=0)
            lane = lax.broadcasted_iota(jnp.int32, whole.shape, 1)
            yp = jnp.where(lane < members, whole, 0.0)
            hi = yp.astype(jnp.bfloat16).astype(jnp.float32)
            lo = yp - hi
            lo_at = pltpu.roll(lo, members, 1)
            first = jnp.where(lane < members, hi, lo_at)
            second = jnp.where(lane < 2 * members - tcols, lo_at, pltpu.roll(hi, 2 * members - tcols, 1))
            both = jnp.concatenate([first, second], axis=1)
            left[batch] = pad_rows(both, depth).astype(jnp.bfloat16)
            full = -(-depth // tcols) * tcols
            turned = jnp.transpose(pad_rows(whole, full))[:tall]
            alpha = jnp.transpose(pad_rows(whole, full))[members + 2 : members + 3]
            at = lax.broadcasted_iota(jnp.int32, turned.shape, 0)
            scaled = jnp.where(at < members, -alpha * turned, jnp.where(at == members, turned, 0.0))
            hi, lo = split(scaled)
            back[batch, 0:tall] = hi[:, :depth]
            back[batch, tall:] = lo[:, :depth]
            column = lax.broadcasted_iota(jnp.int32, whole.shape, 1).astype(jnp.float32)
            near_w = taper((cols - column) / trows) * (factor * (1.0 / (members - 1)))
            colw[batch] = pad_rows(near_w, depth)
            rowrel[batch] = pad_rows(jnp.broadcast_to(rows, whole.shape), depth)

    lines = out_ref.reshape(fields * members * high, tcols)
    zeros = jnp.zeros((wide - 3 * members, 2 * tcols), jnp.bfloat16)

    def pair(p, carry):
        row = step * high + 2 * p
        loc = []
        for batch in range(2):
            parts = []
            for d in range(2):
                z = (rowrel[batch] - (row + d).astype(jnp.float32)) * (1.0 / trows)
                parts.append(taper(z) * colw[batch])
            loc.append(jnp.concatenate(parts, axis=1))
        for f in range(fields):
            x = jnp.concatenate([state_ref[f, 2 * p], state_ref[f, 2 * p + 1]], axis=1)
            mean = jnp.sum(x, axis=0, keepdims=True) * (1.0 / members)
            pert = x - mean
            for batch in range(2):
                hi, lo = split(pert)
                right = jnp.concatenate([hi, hi, lo, zeros], axis=0)
                proj = jnp.dot(left[batch], right, preferred_element_type=jnp.float32)
                w_hi, w_lo = split(proj * loc[batch])
                one = jnp.dot(back[batch], w_hi, preferred_element_type=jnp.float32)
                two = jnp.dot(back[batch, 0:tall], w_lo, preferred_element_type=jnp.float32)
                change = one[:tall] + one[tall:] + two
                pert = pert + change[:members]
                mean = mean + change[members : members + 1]
            x = mean + pert
            for d in range(2):
                lines[pl.ds(f * members * high + 2 * p + d, members, stride=high), :] = x[:, d * tcols : (d + 1) * tcols]
        return carry

    lax.fori_loop(0, high // 2, pair, 0)


def on_device(n_lat, n_lon, ensemble, courant_cols, courant_rows, obs_value, obs_error, obs_cell, obs_kind, obs_live, obs_list):
    fields, members, trows, tcols = ensemble.shape
    slots = obs_value.shape[1]
    f32 = jnp.float32
    row, col = obs_cell // tcols, obs_cell % tcols
    info = jnp.concatenate(
        [jnp.stack([obs_value, obs_live.astype(f32), obs_error, row.astype(f32), col.astype(f32)], axis=1),
         jnp.swapaxes(obs_list, 1, 2).astype(f32)], axis=1)
    info = jnp.pad(info, ((0, 0), (0, EXTRA - info.shape[1]), (0, tcols - slots)), constant_values=1.0)
    place = jnp.stack([obs_kind * trows + row, col], axis=1)
    vmem = pl.BlockSpec(memory_space=pltpu.VMEM)
    state, tables = pl.pallas_call(
        functools.partial(exchange_kernel, (fields, members, trows, tcols, slots, n_lat, n_lon)),
        out_shape=(
            jax.ShapeDtypeStruct((fields * trows, members, tcols), f32),
            jax.ShapeDtypeStruct((2, 9, slots, tcols), f32),
        ),
        in_specs=[vmem] * 4 + [pl.BlockSpec(memory_space=pltpu.SMEM)],
        out_specs=(vmem, vmem),
        scratch_shapes=[
            pltpu.VMEM((fields, trows + 2, members, tcols), f32),
            pltpu.VMEM((2, members, tcols), f32),
            pltpu.VMEM((2, members, tcols), f32),
            pltpu.VMEM((2, 9, slots, tcols), f32),
        ] + [pltpu.SemaphoreType.DMA((2,))] * 4 + [pltpu.SemaphoreType.DMA((2, 9))] * 2,
        compiler_params=pltpu.CompilerParams(
            collective_id=0, has_side_effects=True, vmem_limit_bytes=40 * 2**20),
        name="exchange",
    )(ensemble.reshape(fields * members * trows, tcols), courant_cols[0], courant_rows[0], info, place)

    high = 8
    depth = -(-9 * slots // 16) * 16
    tall = -(-(members + 1) // 16) * 16
    wide = -(-3 * members // tcols) * tcols
    return pl.pallas_call(
        functools.partial(update_kernel, (fields, members, trows, tcols, slots, high)),
        grid=(trows // high,),
        out_shape=jax.ShapeDtypeStruct(ensemble.shape, f32),
        in_specs=[
            pl.BlockSpec((fields, high, members, tcols), lambda i: (0, i, 0, 0)),
            pl.BlockSpec((2, 9, slots, tcols), lambda i: (0, 0, 0, 0)),
        ],
        out_specs=pl.BlockSpec((fields, members, high, tcols), lambda i: (0, 0, i, 0)),
        scratch_shapes=[
            pltpu.VMEM((2, depth, wide), jnp.bfloat16),
            pltpu.VMEM((2, 2 * tall, depth), jnp.bfloat16),
            pltpu.VMEM((2, depth, tcols), f32),
            pltpu.VMEM((2, depth, tcols), f32),
        ],
        compiler_params=pltpu.CompilerParams(vmem_limit_bytes=40 * 2**20),
        name="update",
    )(state.reshape(fields, trows, members, tcols), tables)


def solution(mesh):
    placed = (
        P(None, None, "lat", "lon"),
        P(None, "lat", "lon"),
        P(None, "lat", "lon"),
        P(None, ("lat", "lon")),
        P(None, ("lat", "lon")),
        P(None, ("lat", "lon")),
        P(None, ("lat", "lon")),
        P(None, ("lat", "lon")),
        P(None, ("lat", "lon"), None),
    )
    return jax.shard_map(
        functools.partial(on_device, mesh.shape["lat"], mesh.shape["lon"]),
        mesh=mesh,
        in_specs=placed,
        out_specs=P(None, None, "lat", "lon"),
        check_vma=False,
    )
```

```python
import functools
import jax
import jax.numpy as jnp
from jax import lax
from jax.sharding import PartitionSpec as P
from jax.experimental import pallas as pl
from jax.experimental.pallas import tpu as pltpu

MESH = pl.DeviceIdType.MESH
EXTRA = 16
HIGHEST = lax.Precision.HIGHEST
AROUND = [(a, b) for a in (-1, 0, 1) for b in (-1, 0, 1) if (a, b) != (0, 0)]


def slot_of(a, b):
    return (a + 1) * 3 + b + 1


def taper(dist):
    return jnp.square(jnp.maximum(0.0, 1.0 - jnp.abs(dist)))


def pad_rows(x, rows):
    if rows == x.shape[0]:
        return x
    return jnp.concatenate([x, jnp.zeros((rows - x.shape[0], x.shape[1]), x.dtype)], axis=0)


def table_columns(near, members, trows, tcols):
    rows, cols, factor = [], [], []
    for a in (-1, 0, 1):
        for b in (-1, 0, 1):
            block = near[slot_of(a, b)]
            rows.append(block[:, members + 3 : members + 4] + float(a * trows))
            cols.append(block[:, members + 4 : members + 5] + float(b * tcols))
            took = members + 5 + slot_of(-a, -b)
            factor.append(block[:, members + 1 : members + 2] * block[:, took : took + 1])
    return [jnp.concatenate(part, axis=0) for part in (rows, cols, factor)]


def make_table(prior, info):
    members, lanes = prior.shape
    ybar = jnp.sum(prior, axis=0, keepdims=True) / members
    yp = prior - ybar
    spread = jnp.sum(yp * yp, axis=0, keepdims=True) / (members - 1)
    value, live, error = info[0:1], info[1:2], info[2:3]
    total = spread + error
    gain = live / total
    alpha = 1.0 / (1.0 + jnp.sqrt(error / total))
    innov = value - ybar
    at = lax.broadcasted_iota(jnp.int32, info.shape, 0)
    extra = jnp.where(at == 0, innov, jnp.where(at == 1, gain, jnp.where(at == 2, alpha, info)))
    return jnp.transpose(pad_rows(jnp.concatenate([yp, extra], axis=0), lanes))


def exchange_kernel(
    sizes, x_hbm, cu_hbm, cv_hbm, value_hbm, error_hbm, live_hbm, cell_hbm, list_hbm, cell_ref, kind_ref,
    state_ref, sides_ref, tables_ref,
    x_ref, cu_ref, cv_ref, value_ref, error_ref, live_ref, cells_ref, list_ref, info, listed,
    xt, pack, halo, near, in_sem, row_send, row_recv, col_send, col_recv, tab_send, tab_recv,
):
    fields, members, trows, tcols, slots, n_lat, n_lon = sizes
    lat, lon = lax.axis_index("lat"), lax.axis_index("lon")

    def exists(a, b):
        r, c = lat + a, lon + b
        return (r >= 0) & (r < n_lat) & (c >= 0) & (c < n_lon)

    loads = [
        pltpu.make_async_copy(src, dst, in_sem.at[k])
        for k, (src, dst) in enumerate([
            (x_hbm, x_ref), (cu_hbm, cu_ref), (cv_hbm, cv_ref), (value_hbm, value_ref), (error_hbm, error_ref),
            (live_hbm, live_ref), (cell_hbm, cells_ref), (list_hbm, list_ref)])
    ]
    for copy in loads:
        copy.start()

    xt[:, 0] = jnp.zeros((fields, members, tcols), jnp.float32)
    xt[:, trows + 1] = jnp.zeros((fields, members, tcols), jnp.float32)
    halo[...] = jnp.zeros(halo.shape, jnp.float32)
    near[...] = jnp.zeros(near.shape, jnp.float32)
    info[...] = jnp.ones(info.shape, jnp.float32)
    listed[...] = jnp.zeros(listed.shape, jnp.float32)

    barrier = pltpu.get_barrier_semaphore()
    for a, b in AROUND:
        @pl.when(exists(a, b))
        def _():
            pl.semaphore_signal(barrier, inc=1, device_id=(lat + a, lon + b), device_id_type=MESH)

    lane = lax.broadcasted_iota(jnp.int32, (members, tcols), 1)
    for copy in loads:
        copy.wait()

    def turn(i, carry):
        west, east = carry
        for f in range(fields):
            tile = x_ref[pl.ds(f * members * trows + i, members, stride=trows), :]
            xt[f, i + 1] = tile
            here = lane == f * trows + i
            west = jnp.where(here, jnp.broadcast_to(tile[:, 0:1], tile.shape), west)
            east = jnp.where(here, jnp.broadcast_to(tile[:, tcols - 1 : tcols], tile.shape), east)
        return west, east

    none = jnp.zeros((members, tcols), jnp.float32)
    west, east = lax.fori_loop(0, trows, turn, (none, none), unroll=2)
    pack[0] = west
    pack[1] = east

    lat_n = jnp.where(lat > 0, 1, 0) + jnp.where(lat < n_lat - 1, 1, 0) + 1
    lon_n = jnp.where(lon > 0, 1, 0) + jnp.where(lon < n_lon - 1, 1, 0) + 1
    pl.semaphore_wait(barrier, lat_n * lon_n - 1)

    def row_copy(k):
        return pltpu.make_async_remote_copy(
            src_ref=xt.at[:, 1 if k == 0 else trows],
            dst_ref=xt.at[:, trows + 1 if k == 0 else 0],
            send_sem=row_send.at[k], recv_sem=row_recv.at[k],
            device_id=(lat - 1 if k == 0 else lat + 1, lon), device_id_type=MESH,
        )

    def col_copy(k):
        return pltpu.make_async_remote_copy(
            src_ref=pack.at[k], dst_ref=halo.at[k],
            send_sem=col_send.at[k], recv_sem=col_recv.at[k],
            device_id=(lat, lon - 1 if k == 0 else lon + 1), device_id_type=MESH,
        )

    for k, d in ((0, -1), (1, 1)):
        @pl.when(exists(0, d))
        def _():
            col_copy(k).start()

        @pl.when(exists(d, 0))
        def _():
            row_copy(k).start()

    def advect(i, carry):
        u = jnp.broadcast_to(cu_ref[0, pl.ds(i, 1), :], (members, tcols))
        v = jnp.broadcast_to(cv_ref[0, pl.ds(i, 1), :], (members, tcols))
        hu, hv = 0.5 * u, 0.5 * v
        huu, hvv = hu * u, hv * v
        for f in range(fields):
            mid = xt[f, i + 1]
            south = xt[f, i]
            north = xt[f, i + 2]
            east = jnp.where(lane == tcols - 1, 0.0, pltpu.roll(mid, tcols - 1, 1))
            west = jnp.where(lane == 0, 0.0, pltpu.roll(mid, 1, 1))
            two = 2.0 * mid
            out = mid - hu * (east - west) + huu * (east - two + west)
            out = out - hv * (north - south) + hvv * (north - two + south)
            state_ref[f * trows + i] = out
        return carry

    lax.fori_loop(1, trows - 1, advect, 0)

    for batch in range(2):
        own = pl.ds(0, slots)
        cells = cells_ref[batch : batch + 1, :]
        info[batch, 0:1, own] = value_ref[batch : batch + 1, :]
        info[batch, 1:2, own] = live_ref[batch : batch + 1, :].astype(jnp.float32)
        info[batch, 2:3, own] = error_ref[batch : batch + 1, :]
        row = jnp.floor((cells.astype(jnp.float32) + 0.5) * (1.0 / tcols))
        info[batch, 3:4, own] = row
        info[batch, 4:5, own] = cells.astype(jnp.float32) - row * tcols
        listed[batch, :, 0 : list_ref.shape[2]] = list_ref[batch].astype(jnp.float32)

    def along(column):
        spread = jnp.broadcast_to(column, (trows, tcols))
        line = jnp.transpose(pad_rows(spread, tcols))[0:1]
        total = line
        for f in range(1, fields):
            total = total + pltpu.roll(jnp.broadcast_to(line, (8, tcols)), f * trows, 1)[0:1]
        return total

    u = cu_ref[0]
    rise = along((0.5 * u + 0.5 * u * u)[:, 0:1])
    fall = along((0.5 * u * u - 0.5 * u)[:, tcols - 1 : tcols])

    for k, d in ((0, -1), (1, 1)):
        @pl.when(exists(0, d))
        def _():
            col_copy(k).wait_send()

        @pl.when(exists(d, 0))
        def _():
            row_copy(k).wait_send()

        @pl.when(exists(0, -d))
        def _():
            col_copy(k).wait_recv()

        @pl.when(exists(-d, 0))
        def _():
            row_copy(k).wait_recv()

    advect(0, 0)
    advect(trows - 1, 0)
    first_add = halo[1] * rise
    last_add = halo[0] * fall
    sides_ref[0] = first_add
    sides_ref[1] = last_add

    def gather(batch):
        prior = none
        for s in range(slots):
            cell = cell_ref[batch, s]
            col = lax.rem(cell, tcols)
            at = kind_ref[batch, s] * trows + lax.div(cell, tcols)
            tile = state_ref[at]
            here = lane == at
            picked = jnp.where(lane == col, tile, 0.0)
            picked = picked + jnp.where(here & (col == 0), first_add, 0.0)
            picked = picked + jnp.where(here & (col == tcols - 1), last_add, 0.0)
            column = jnp.sum(picked, axis=1, keepdims=True)
            prior = jnp.where(lane == s, jnp.broadcast_to(column, tile.shape), prior)
        return prior

    def table_copy(batch, a, b):
        return pltpu.make_async_remote_copy(
            src_ref=near.at[batch, slot_of(0, 0)],
            dst_ref=near.at[batch, slot_of(-a, -b)],
            send_sem=tab_send.at[batch, slot_of(a, b)],
            recv_sem=tab_recv.at[batch, slot_of(-a, -b)],
            device_id=(lat + a, lon + b), device_id_type=MESH,
        )

    def send(batch, prior):
        table = make_table(prior, info[batch])[:slots]
        at = lax.broadcasted_iota(jnp.int32, table.shape, 1)
        table = jnp.where(at < members + 5, table, pltpu.roll(listed[batch], members + 5, 1))
        near[batch, slot_of(0, 0)] = table
        for a, b in AROUND:
            @pl.when(exists(a, b))
            def _():
                table_copy(batch, a, b).start()

    def finish(batch):
        for a, b in AROUND:
            @pl.when(exists(a, b))
            def _():
                table_copy(batch, a, b).wait_send()

            @pl.when(exists(-a, -b))
            def _():
                table_copy(batch, a, b).wait_recv()

    send(0, gather(0))
    later = gather(1)
    finish(0)

    board = [near[0, k] for k in range(9)]
    rows, cols, factor = table_columns(board, members, trows, tcols)
    whole = jnp.concatenate(board, axis=0)
    count = whole.shape[0]
    loc = taper((rows - info[1, 3:4]) / trows) * factor * taper((cols - info[1, 4:5]) / trows)
    mean = jnp.sum(later, axis=0, keepdims=True) / members
    pert = later - mean
    shut = lax.broadcasted_iota(jnp.int32, whole.shape, 1)
    yp = jnp.where(shut < members, whole, 0.0)
    proj = jnp.dot(yp, pad_rows(pert, tcols), precision=HIGHEST, preferred_element_type=jnp.float32)
    weight = proj * loc * (1.0 / (members - 1))
    mean = mean + jnp.sum(weight * whole[:, members : members + 1], axis=0, keepdims=True)
    scaled = whole * whole[:, members + 2 : members + 3]
    full = -(-count // tcols) * tcols
    change = jnp.dot(
        jnp.transpose(pad_rows(scaled, full))[:members], pad_rows(weight, full),
        precision=HIGHEST, preferred_element_type=jnp.float32,
    )
    send(1, mean + pert - change)
    finish(1)
    tables_ref[...] = near[...]


def split(x):
    hi = x.astype(jnp.bfloat16)
    return hi, (x - hi.astype(jnp.float32)).astype(jnp.bfloat16)


def beside(parts, rows, lanes):
    width = parts[0][1]
    total = [jnp.zeros((rows, lanes), jnp.float32) for _ in range(2)]
    at = lax.broadcasted_iota(jnp.int32, (rows, lanes), 1)
    for k, (part, _) in enumerate(parts):
        start = k * width
        turned = pltpu.roll(part, start % lanes, 1) if start % lanes else part
        for block in range(2):
            lower, upper = start - block * lanes, start + width - block * lanes
            if upper > 0 and lower < lanes:
                total[block] = jnp.where((at >= lower) & (at < upper), turned, total[block])
    return jnp.concatenate(total, axis=1)


def update_kernel(sizes, state_ref, sides_ref, tables_ref, out_ref, left, back, back3, back2, rowrel, colw, active_ref):
    fields, members, trows, tcols, slots, high = sizes
    depth = left.shape[1]
    wide = left.shape[2]
    tall = back.shape[1] // 2
    third = 2 * tcols // 48 * 16
    step = pl.program_id(0)

    @pl.when(step == 0)
    def _():
        for batch in range(2):
            board = [tables_ref[batch, k] for k in range(9)]
            rows, cols, factor = table_columns(board, members, trows, tcols)
            whole = jnp.concatenate(board, axis=0)
            lane = lax.broadcasted_iota(jnp.int32, whole.shape, 1)
            reach = (
                (factor != 0.0) & (rows > -trows) & (rows < 2 * trows - 1)
                & (cols > -trows) & (cols < tcols - 1 + trows)
            )
            active = jnp.where(reach, 1.0, 0.0)
            whole = jnp.where(lane == members + 1, factor * (1.0 / (members - 1)), whole)
            whole = jnp.where(lane == members + 3, rows, whole)
            whole = jnp.where(lane == members + 4, cols, whole)
            whole = jnp.where(lane == members + 5, active, whole)
            full = -(-depth // tcols) * tcols
            whole = pad_rows(whole, full)
            flags = jnp.transpose(whole)[members + 5 : members + 6]
            r = lax.broadcasted_iota(jnp.int32, (full, full), 0)
            c = lax.broadcasted_iota(jnp.int32, (full, full), 1)
            upper = jnp.where(r <= c, 1.0, 0.0).astype(jnp.bfloat16)
            line = jnp.broadcast_to(flags, (16, full)).astype(jnp.bfloat16)
            running = jnp.dot(line, upper, preferred_element_type=jnp.float32)[0:1]
            active_ref[batch] = jnp.max(running).astype(jnp.int32)
            pick = jnp.where((running - 1.0 == r.astype(jnp.float32)) & (flags > 0.5), 1.0, 0.0)
            whole = jnp.dot(pick, whole, precision=HIGHEST, preferred_element_type=jnp.float32)

            lane = lax.broadcasted_iota(jnp.int32, whole.shape, 1)
            yp = jnp.where(lane < members, whole, 0.0)
            hi = yp.astype(jnp.bfloat16).astype(jnp.float32)
            lo = yp - hi
            both = beside([(hi, members), (lo, members), (hi, members)], full, tcols)
            left[batch] = both[:depth].astype(jnp.bfloat16)
            turned = jnp.transpose(whole)
            alpha = turned[members + 2 : members + 3]
            turned = turned[:tall]
            at = lax.broadcasted_iota(jnp.int32, turned.shape, 0)
            scaled = jnp.where(at < members, -alpha * turned, jnp.where(at == members, turned, 0.0))
            hi, lo = split(scaled)
            back[batch, 0:tall] = hi[:, :depth]
            back[batch, tall:] = lo[:, :depth]
            hi = hi.astype(jnp.float32)[:, :tcols]
            lo = lo.astype(jnp.float32)[:, :tcols]
            back3[batch] = beside([(hi, third), (lo, third), (hi, third)], tall, tcols).astype(jnp.bfloat16)
            back2[batch, 0:tall] = jnp.concatenate([hi, hi], axis=1).astype(jnp.bfloat16)
            back2[batch, tall:] = jnp.concatenate([lo, jnp.zeros_like(lo)], axis=1).astype(jnp.bfloat16)
            column = lane.astype(jnp.float32)
            near_w = taper((whole[:, members + 4 : members + 5] - column) / trows) * whole[:, members + 1 : members + 2]
            colw[batch] = near_w[:depth]
            rowrel[batch] = jnp.broadcast_to(whole[:, members + 3 : members + 4], whole.shape)[:depth]

    lines = out_ref.reshape(fields * members * high, tcols)
    lane = lax.broadcasted_iota(jnp.int32, (members, tcols), 1)

    def run(taken):
        def zero_rows(rows):
            return [jnp.zeros((rows, 2 * tcols), jnp.bfloat16)] if rows else []

        def pair(p, carry):
            row = step * high + 2 * p
            loc = []
            for batch in range(2):
                parts = []
                for d in range(2):
                    z = (rowrel[batch, 0:taken] - (row + d).astype(jnp.float32)) * (1.0 / trows)
                    parts.append(taper(z) * colw[batch, 0:taken])
                loc.append(jnp.concatenate(parts, axis=1))
            xs = []
            for f in range(fields):
                tiles = []
                for d in range(2):
                    at = f * trows + row + d
                    first = pltpu.roll(sides_ref[0], lax.rem(tcols - at, tcols), 1)
                    last = pltpu.roll(sides_ref[1], tcols - 1 - at, 1)
                    add = jnp.where(lane == 0, first, jnp.where(lane == tcols - 1, last, 0.0))
                    tiles.append(state_ref[f, 2 * p + d] + add)
                xs.append(jnp.concatenate(tiles, axis=1))
            means = [jnp.sum(x, axis=0, keepdims=True) * (1.0 / members) for x in xs]
            perts = [x - mean for x, mean in zip(xs, means)]
            for batch in range(2):
                projs = []
                for f in range(fields):
                    hi, lo = split(perts[f])
                    right = jnp.concatenate([hi, hi, lo] + zero_rows(wide - 3 * members), axis=0)
                    projs.append(jnp.dot(left[batch, 0:taken], right, preferred_element_type=jnp.float32))
                for f in range(fields):
                    w_hi, w_lo = split(projs[f] * loc[batch])
                    if taken == third:
                        stack = jnp.concatenate([w_hi, w_hi, w_lo] + zero_rows(2 * tcols - 3 * third), axis=0)
                        change = jnp.dot(back3[batch], stack, preferred_element_type=jnp.float32)
                    elif taken == tcols:
                        stack = jnp.concatenate([w_hi, w_lo], axis=0)
                        one = jnp.dot(back2[batch], stack, preferred_element_type=jnp.float32)
                        change = one[:tall] + one[tall:]
                    else:
                        one = jnp.dot(back[batch], w_hi, preferred_element_type=jnp.float32)
                        two = jnp.dot(back[batch, 0:tall], w_lo, preferred_element_type=jnp.float32)
                        change = one[:tall] + one[tall:] + two
                    perts[f] = perts[f] + change[:members]
                    means[f] = means[f] + change[members : members + 1]
            for f in range(fields):
                x = means[f] + perts[f]
                for d in range(2):
                    lines[pl.ds(f * members * high + 2 * p + d, members, stride=high), :] = x[:, d * tcols : (d + 1) * tcols]
            return carry

        lax.fori_loop(0, high // 2, pair, 0)

    most = jnp.maximum(active_ref[0], active_ref[1])

    @pl.when(most <= third)
    def _():
        run(third)

    @pl.when((most > third) & (most <= tcols))
    def _():
        run(tcols)

    @pl.when(most > tcols)
    def _():
        run(depth)


def on_device(n_lat, n_lon, ensemble, courant_cols, courant_rows, obs_value, obs_error, obs_cell, obs_kind, obs_live, obs_list):
    fields, members, trows, tcols = ensemble.shape
    slots = obs_value.shape[1]
    f32, i32 = jnp.float32, jnp.int32
    vmem = pl.BlockSpec(memory_space=pltpu.VMEM)
    smem = pl.BlockSpec(memory_space=pltpu.SMEM)
    lines = ensemble.reshape(fields * members * trows, tcols)
    raw = (lines, courant_cols, courant_rows, obs_value, obs_error, obs_live, obs_cell, obs_list)
    state, sides, tables = pl.pallas_call(
        functools.partial(exchange_kernel, (fields, members, trows, tcols, slots, n_lat, n_lon)),
        out_shape=(
            jax.ShapeDtypeStruct((fields * trows, members, tcols), f32),
            jax.ShapeDtypeStruct((2, members, tcols), f32),
            jax.ShapeDtypeStruct((2, 9, slots, tcols), f32),
        ),
        in_specs=[pl.BlockSpec(memory_space=pl.ANY)] * len(raw) + [smem, smem],
        out_specs=(vmem, vmem, vmem),
        scratch_shapes=[pltpu.VMEM(part.shape, part.dtype) for part in raw] + [
            pltpu.VMEM((2, EXTRA, tcols), f32),
            pltpu.VMEM((2, slots, tcols), f32),
            pltpu.VMEM((fields, trows + 2, members, tcols), f32),
            pltpu.VMEM((2, members, tcols), f32),
            pltpu.VMEM((2, members, tcols), f32),
            pltpu.VMEM((2, 9, slots, tcols), f32),
            pltpu.SemaphoreType.DMA((len(raw),)),
        ] + [pltpu.SemaphoreType.DMA((2,))] * 4 + [pltpu.SemaphoreType.DMA((2, 9))] * 2,
        compiler_params=pltpu.CompilerParams(
            collective_id=0, has_side_effects=True, vmem_limit_bytes=40 * 2**20),
        name="exchange",
    )(*raw, obs_cell, obs_kind)

    high = 8
    depth = -(-9 * slots // 16) * 16
    tall = -(-(members + 1) // 16) * 16
    wide = -(-3 * members // tcols) * tcols
    return pl.pallas_call(
        functools.partial(update_kernel, (fields, members, trows, tcols, slots, high)),
        grid=(trows // high,),
        out_shape=jax.ShapeDtypeStruct(ensemble.shape, f32),
        in_specs=[
            pl.BlockSpec((fields, high, members, tcols), lambda i: (0, i, 0, 0)),
            pl.BlockSpec((2, members, tcols), lambda i: (0, 0, 0)),
            pl.BlockSpec((2, 9, slots, tcols), lambda i: (0, 0, 0, 0)),
        ],
        out_specs=pl.BlockSpec((fields, members, high, tcols), lambda i: (0, 0, i, 0)),
        scratch_shapes=[
            pltpu.VMEM((2, depth, wide), jnp.bfloat16),
            pltpu.VMEM((2, 2 * tall, depth), jnp.bfloat16),
            pltpu.VMEM((2, tall, 2 * tcols), jnp.bfloat16),
            pltpu.VMEM((2, 2 * tall, 2 * tcols), jnp.bfloat16),
            pltpu.VMEM((2, depth, tcols), f32),
            pltpu.VMEM((2, depth, tcols), f32),
            pltpu.SMEM((2,), i32),
        ],
        compiler_params=pltpu.CompilerParams(vmem_limit_bytes=40 * 2**20),
        name="update",
    )(state.reshape(fields, trows, members, tcols), sides, tables)


def solution(mesh):
    placed = (
        P(None, None, "lat", "lon"),
        P(None, "lat", "lon"),
        P(None, "lat", "lon"),
        P(None, ("lat", "lon")),
        P(None, ("lat", "lon")),
        P(None, ("lat", "lon")),
        P(None, ("lat", "lon")),
        P(None, ("lat", "lon")),
        P(None, ("lat", "lon"), None),
    )
    return jax.shard_map(
        functools.partial(on_device, mesh.shape["lat"], mesh.shape["lon"]),
        mesh=mesh,
        in_specs=placed,
        out_specs=P(None, None, "lat", "lon"),
        check_vma=False,
    )
```

```python
import functools
import jax
import jax.numpy as jnp
from jax import lax
from jax.sharding import PartitionSpec as P
from jax.experimental import pallas as pl
from jax.experimental.pallas import tpu as pltpu

MESH = pl.DeviceIdType.MESH
EXTRA = 16
HIGHEST = lax.Precision.HIGHEST
AROUND = [(a, b) for a in (-1, 0, 1) for b in (-1, 0, 1) if (a, b) != (0, 0)]


def slot_of(a, b):
    return (a + 1) * 3 + b + 1


def taper(dist):
    return jnp.square(jnp.maximum(0.0, 1.0 - jnp.abs(dist)))


def pad_rows(x, rows):
    if rows == x.shape[0]:
        return x
    return jnp.concatenate([x, jnp.zeros((rows - x.shape[0], x.shape[1]), x.dtype)], axis=0)


def table_columns(near, members, trows, tcols):
    rows, cols, factor = [], [], []
    for a in (-1, 0, 1):
        for b in (-1, 0, 1):
            block = near[slot_of(a, b)]
            rows.append(block[:, members + 3 : members + 4] + float(a * trows))
            cols.append(block[:, members + 4 : members + 5] + float(b * tcols))
            took = members + 5 + slot_of(-a, -b)
            factor.append(block[:, members + 1 : members + 2] * block[:, took : took + 1])
    return [jnp.concatenate(part, axis=0) for part in (rows, cols, factor)]


def make_table(prior, info):
    members, lanes = prior.shape
    ybar = jnp.sum(prior, axis=0, keepdims=True) / members
    yp = prior - ybar
    spread = jnp.sum(yp * yp, axis=0, keepdims=True) / (members - 1)
    value, live, error = info[0:1], info[1:2], info[2:3]
    total = spread + error
    gain = live / total
    alpha = 1.0 / (1.0 + jnp.sqrt(error / total))
    innov = value - ybar
    at = lax.broadcasted_iota(jnp.int32, info.shape, 0)
    extra = jnp.where(at == 0, innov, jnp.where(at == 1, gain, jnp.where(at == 2, alpha, info)))
    return jnp.transpose(pad_rows(jnp.concatenate([yp, extra], axis=0), lanes))


def exchange_kernel(
    sizes, x_hbm, cu_hbm, cv_hbm, value_hbm, error_hbm, live_hbm, cell_hbm, list_hbm, cell_ref, kind_ref,
    state_hbm, sides_ref, tables_ref,
    state_ref, x_ref, cu_ref, cv_ref, value_ref, error_ref, live_ref, cells_ref, list_ref, info,
    xt, pack, halo, near, in_sem, row_send, row_recv, col_send, col_recv, tab_send, tab_recv, out_sem,
):
    fields, members, trows, tcols, slots, n_lat, n_lon = sizes
    lat, lon = lax.axis_index("lat"), lax.axis_index("lon")

    def exists(a, b):
        r, c = lat + a, lon + b
        return (r >= 0) & (r < n_lat) & (c >= 0) & (c < n_lon)

    part = members * trows
    own_field = [pl.ds(f * part, part) for f in range(fields)]
    loads = [
        pltpu.make_async_copy(src, dst, in_sem.at[k])
        for k, (src, dst) in enumerate([(x_hbm.at[own], x_ref.at[own]) for own in own_field] + [
            (cu_hbm, cu_ref), (cv_hbm, cv_ref), (value_hbm, value_ref), (error_hbm, error_ref),
            (live_hbm, live_ref), (cell_hbm, cells_ref), (list_hbm, list_ref)])
    ]
    for copy in loads:
        copy.start()

    xt[:, 0] = jnp.zeros((fields, members, tcols), jnp.float32)
    xt[:, trows + 1] = jnp.zeros((fields, members, tcols), jnp.float32)
    halo[...] = jnp.zeros(halo.shape, jnp.float32)
    near[...] = jnp.zeros(near.shape, jnp.float32)
    info[...] = jnp.ones(info.shape, jnp.float32)

    barrier = pltpu.get_barrier_semaphore()
    for a, b in AROUND:
        @pl.when(exists(a, b))
        def _():
            pl.semaphore_signal(barrier, inc=1, device_id=(lat + a, lon + b), device_id_type=MESH)

    lane = lax.broadcasted_iota(jnp.int32, (members, tcols), 1)

    def turn(f, i, carry):
        west, east = carry
        tile = x_ref[pl.ds(f * part + i, members, stride=trows), :]
        xt[f, i + 1] = tile
        here = lane == f * trows + i
        west = jnp.where(here, jnp.broadcast_to(tile[:, 0:1], tile.shape), west)
        east = jnp.where(here, jnp.broadcast_to(tile[:, tcols - 1 : tcols], tile.shape), east)
        return west, east

    none = jnp.zeros((members, tcols), jnp.float32)
    west, east = none, none
    for f in range(fields):
        loads[f].wait()
        west, east = lax.fori_loop(0, trows, functools.partial(turn, f), (west, east), unroll=4)
    pack[0] = west
    pack[1] = east

    lat_n = jnp.where(lat > 0, 1, 0) + jnp.where(lat < n_lat - 1, 1, 0) + 1
    lon_n = jnp.where(lon > 0, 1, 0) + jnp.where(lon < n_lon - 1, 1, 0) + 1
    pl.semaphore_wait(barrier, lat_n * lon_n - 1)

    def row_copy(k):
        return pltpu.make_async_remote_copy(
            src_ref=xt.at[:, 1 if k == 0 else trows],
            dst_ref=xt.at[:, trows + 1 if k == 0 else 0],
            send_sem=row_send.at[k], recv_sem=row_recv.at[k],
            device_id=(lat - 1 if k == 0 else lat + 1, lon), device_id_type=MESH,
        )

    def col_copy(k):
        return pltpu.make_async_remote_copy(
            src_ref=pack.at[k], dst_ref=halo.at[k],
            send_sem=col_send.at[k], recv_sem=col_recv.at[k],
            device_id=(lat, lon - 1 if k == 0 else lon + 1), device_id_type=MESH,
        )

    for k, d in ((0, -1), (1, 1)):
        @pl.when(exists(0, d))
        def _():
            col_copy(k).start()

        @pl.when(exists(d, 0))
        def _():
            row_copy(k).start()

    for copy in loads[fields:]:
        copy.wait()

    def advect(i, carry):
        u = jnp.broadcast_to(cu_ref[0, pl.ds(i, 1), :], (members, tcols))
        v = jnp.broadcast_to(cv_ref[0, pl.ds(i, 1), :], (members, tcols))
        hu, hv = 0.5 * u, 0.5 * v
        huu, hvv = hu * u, hv * v
        for f in range(fields):
            mid = xt[f, i + 1]
            south = xt[f, i]
            north = xt[f, i + 2]
            east = jnp.where(lane == tcols - 1, 0.0, pltpu.roll(mid, tcols - 1, 1))
            west = jnp.where(lane == 0, 0.0, pltpu.roll(mid, 1, 1))
            two = 2.0 * mid
            out = mid - hu * (east - west) + huu * (east - two + west)
            out = out - hv * (north - south) + hvv * (north - two + south)
            state_ref[f * trows + i] = out
        return carry

    lax.fori_loop(1, trows - 1, advect, 0, unroll=2)

    for batch in range(2):
        own = pl.ds(0, slots)
        cells = cells_ref[batch : batch + 1, :]
        info[batch, 0:1, own] = value_ref[batch : batch + 1, :]
        info[batch, 1:2, own] = live_ref[batch : batch + 1, :].astype(jnp.float32)
        info[batch, 2:3, own] = error_ref[batch : batch + 1, :]
        row = jnp.floor((cells.astype(jnp.float32) + 0.5) * (1.0 / tcols))
        info[batch, 3:4, own] = row
        info[batch, 4:5, own] = cells.astype(jnp.float32) - row * tcols
        for k in range(list_ref.shape[0]):
            info[batch, 5 + k : 6 + k, own] = list_ref[k, batch : batch + 1, :].astype(jnp.float32)

    def along(column):
        spread = jnp.broadcast_to(column, (trows, tcols))
        line = jnp.transpose(pad_rows(spread, tcols))[0:1]
        total = line
        for f in range(1, fields):
            total = total + pltpu.roll(jnp.broadcast_to(line, (8, tcols)), f * trows, 1)[0:1]
        return total

    u = cu_ref[0]
    rise = along((0.5 * u + 0.5 * u * u)[:, 0:1])
    fall = along((0.5 * u * u - 0.5 * u)[:, tcols - 1 : tcols])

    for k, d in ((0, -1), (1, 1)):
        @pl.when(exists(0, d))
        def _():
            col_copy(k).wait_send()

        @pl.when(exists(d, 0))
        def _():
            row_copy(k).wait_send()

        @pl.when(exists(0, -d))
        def _():
            col_copy(k).wait_recv()

        @pl.when(exists(-d, 0))
        def _():
            row_copy(k).wait_recv()

    advect(0, 0)
    advect(trows - 1, 0)
    keep = pltpu.make_async_copy(state_ref, state_hbm, out_sem)
    keep.start()
    first_add = halo[1] * rise
    last_add = halo[0] * fall
    sides_ref[0] = first_add
    sides_ref[1] = last_add

    def gather(batch):
        prior = none
        for s in range(slots):
            cell = cell_ref[batch, s]
            col = lax.rem(cell, tcols)
            at = kind_ref[batch, s] * trows + lax.div(cell, tcols)
            tile = state_ref[at]
            here = lane == at
            picked = jnp.where(lane == col, tile, 0.0)
            picked = picked + jnp.where(here & (col == 0), first_add, 0.0)
            picked = picked + jnp.where(here & (col == tcols - 1), last_add, 0.0)
            column = jnp.sum(picked, axis=1, keepdims=True)
            prior = jnp.where(lane == s, jnp.broadcast_to(column, tile.shape), prior)
        return prior

    def table_copy(batch, a, b):
        return pltpu.make_async_remote_copy(
            src_ref=near.at[batch, slot_of(0, 0)],
            dst_ref=near.at[batch, slot_of(-a, -b)],
            send_sem=tab_send.at[batch, slot_of(a, b)],
            recv_sem=tab_recv.at[batch, slot_of(-a, -b)],
            device_id=(lat + a, lon + b), device_id_type=MESH,
        )

    def send(batch, prior):
        near[batch, slot_of(0, 0)] = make_table(prior, info[batch])[:slots]
        for a, b in AROUND:
            @pl.when(exists(a, b))
            def _():
                table_copy(batch, a, b).start()

    def finish(batch):
        for a, b in AROUND:
            @pl.when(exists(a, b))
            def _():
                table_copy(batch, a, b).wait_send()

            @pl.when(exists(-a, -b))
            def _():
                table_copy(batch, a, b).wait_recv()

    send(0, gather(0))
    later = gather(1)
    finish(0)

    board = [near[0, k] for k in range(9)]
    rows, cols, factor = table_columns(board, members, trows, tcols)
    whole = jnp.concatenate(board, axis=0)
    count = whole.shape[0]
    loc = taper((rows - info[1, 3:4]) / trows) * factor * taper((cols - info[1, 4:5]) / trows)
    mean = jnp.sum(later, axis=0, keepdims=True) / members
    pert = later - mean
    shut = lax.broadcasted_iota(jnp.int32, whole.shape, 1)
    yp = jnp.where(shut < members, whole, 0.0)
    proj = jnp.dot(yp, pad_rows(pert, tcols), precision=HIGHEST, preferred_element_type=jnp.float32)
    weight = proj * loc * (1.0 / (members - 1))
    mean = mean + jnp.sum(weight * whole[:, members : members + 1], axis=0, keepdims=True)
    scaled = whole * whole[:, members + 2 : members + 3]
    full = -(-count // tcols) * tcols
    change = jnp.dot(
        jnp.transpose(pad_rows(scaled, full))[:members], pad_rows(weight, full),
        precision=HIGHEST, preferred_element_type=jnp.float32,
    )
    send(1, mean + pert - change)
    finish(1)
    tables_ref[...] = near[...]
    keep.wait()


def split(x):
    hi = x.astype(jnp.bfloat16)
    return hi, (x - hi.astype(jnp.float32)).astype(jnp.bfloat16)


def beside(parts, rows, lanes):
    width = parts[0][1]
    total = [jnp.zeros((rows, lanes), jnp.float32) for _ in range(2)]
    at = lax.broadcasted_iota(jnp.int32, (rows, lanes), 1)
    for k, (part, _) in enumerate(parts):
        start = k * width
        turned = pltpu.roll(part, start % lanes, 1) if start % lanes else part
        for block in range(2):
            lower, upper = start - block * lanes, start + width - block * lanes
            if upper > 0 and lower < lanes:
                total[block] = jnp.where((at >= lower) & (at < upper), turned, total[block])
    return jnp.concatenate(total, axis=1)


def update_kernel(sizes, state_ref, sides_ref, tables_ref, out_ref, left, back, back3, back2, rowrel, colw, active_ref):
    fields, members, trows, tcols, slots, high = sizes
    depth = left.shape[1]
    wide = left.shape[2]
    tall = back.shape[1] // 2
    third = 2 * tcols // 48 * 16
    step = pl.program_id(0)

    @pl.when(step == 0)
    def _():
        for batch in range(2):
            board = [tables_ref[batch, k] for k in range(9)]
            rows, cols, factor = table_columns(board, members, trows, tcols)
            whole = jnp.concatenate(board, axis=0)
            lane = lax.broadcasted_iota(jnp.int32, whole.shape, 1)
            reach = (
                (factor != 0.0) & (rows > -trows) & (rows < 2 * trows - 1)
                & (cols > -trows) & (cols < tcols - 1 + trows)
            )
            active = jnp.where(reach, 1.0, 0.0)
            whole = jnp.where(lane == members + 1, factor * (1.0 / (members - 1)), whole)
            whole = jnp.where(lane == members + 3, rows, whole)
            whole = jnp.where(lane == members + 4, cols, whole)
            whole = jnp.where(lane == members + 5, active, whole)
            full = -(-depth // tcols) * tcols
            whole = pad_rows(whole, full)
            flags = jnp.transpose(whole)[members + 5 : members + 6]
            r = lax.broadcasted_iota(jnp.int32, (full, full), 0)
            c = lax.broadcasted_iota(jnp.int32, (full, full), 1)
            upper = jnp.where(r <= c, 1.0, 0.0).astype(jnp.bfloat16)
            line = jnp.broadcast_to(flags, (16, full)).astype(jnp.bfloat16)
            running = jnp.dot(line, upper, preferred_element_type=jnp.float32)[0:1]
            active_ref[batch] = jnp.max(running).astype(jnp.int32)
            pick = jnp.where((running - 1.0 == r.astype(jnp.float32)) & (flags > 0.5), 1.0, 0.0)
            whole = jnp.dot(pick, whole, precision=HIGHEST, preferred_element_type=jnp.float32)

            lane = lax.broadcasted_iota(jnp.int32, whole.shape, 1)
            yp = jnp.where(lane < members, whole, 0.0)
            hi = yp.astype(jnp.bfloat16).astype(jnp.float32)
            lo = yp - hi
            both = beside([(hi, members), (lo, members), (hi, members)], full, tcols)
            left[batch] = both[:depth].astype(jnp.bfloat16)
            turned = jnp.transpose(whole)
            alpha = turned[members + 2 : members + 3]
            turned = turned[:tall]
            at = lax.broadcasted_iota(jnp.int32, turned.shape, 0)
            scaled = jnp.where(at < members, -alpha * turned, jnp.where(at == members, turned, 0.0))
            hi, lo = split(scaled)
            back[batch, 0:tall] = hi[:, :depth]
            back[batch, tall:] = lo[:, :depth]
            hi = hi.astype(jnp.float32)[:, :tcols]
            lo = lo.astype(jnp.float32)[:, :tcols]
            back3[batch] = beside([(hi, third), (lo, third), (hi, third)], tall, tcols).astype(jnp.bfloat16)
            back2[batch, 0:tall] = jnp.concatenate([hi, hi], axis=1).astype(jnp.bfloat16)
            back2[batch, tall:] = jnp.concatenate([lo, jnp.zeros_like(lo)], axis=1).astype(jnp.bfloat16)
            column = lane.astype(jnp.float32)
            near_w = taper((whole[:, members + 4 : members + 5] - column) / trows) * whole[:, members + 1 : members + 2]
            colw[batch] = near_w[:depth]
            rowrel[batch] = jnp.broadcast_to(whole[:, members + 3 : members + 4], whole.shape)[:depth]

    lines = out_ref.reshape(fields * members * high, tcols)
    lane = lax.broadcasted_iota(jnp.int32, (members, tcols), 1)

    def run(taken):
        def zero_rows(rows):
            return [jnp.zeros((rows, 2 * tcols), jnp.bfloat16)] if rows else []

        def pairs(q, carry):
            locs, xs = [], []
            for p in range(together):
                row = step * high + 2 * (together * q + p)
                locs.append([])
                for batch in range(2):
                    parts = []
                    for d in range(2):
                        z = (rowrel[batch, 0:taken] - (row + d).astype(jnp.float32)) * (1.0 / trows)
                        parts.append(taper(z) * colw[batch, 0:taken])
                    locs[p].append(jnp.concatenate(parts, axis=1))
                for f in range(fields):
                    tiles = []
                    for d in range(2):
                        at = f * trows + row + d
                        first = pltpu.roll(sides_ref[0], lax.rem(tcols - at, tcols), 1)
                        last = pltpu.roll(sides_ref[1], tcols - 1 - at, 1)
                        add = jnp.where(lane == 0, first, jnp.where(lane == tcols - 1, last, 0.0))
                        tiles.append(state_ref[f, 2 * (together * q + p) + d] + add)
                    xs.append(jnp.concatenate(tiles, axis=1))
            means = [jnp.sum(x, axis=0, keepdims=True) * (1.0 / members) for x in xs]
            perts = [x - mean for x, mean in zip(xs, means)]
            for batch in range(2):
                projs = []
                for k in range(len(xs)):
                    hi, lo = split(perts[k])
                    right = jnp.concatenate([hi, hi, lo] + zero_rows(wide - 3 * members), axis=0)
                    projs.append(jnp.dot(left[batch, 0:taken], right, preferred_element_type=jnp.float32))
                for k in range(len(xs)):
                    w_hi, w_lo = split(projs[k] * locs[k // fields][batch])
                    if taken == third:
                        stack = jnp.concatenate([w_hi, w_hi, w_lo] + zero_rows(2 * tcols - 3 * third), axis=0)
                        change = jnp.dot(back3[batch], stack, preferred_element_type=jnp.float32)
                    elif taken == tcols:
                        stack = jnp.concatenate([w_hi, w_lo], axis=0)
                        one = jnp.dot(back2[batch], stack, preferred_element_type=jnp.float32)
                        change = one[:tall] + one[tall:]
                    else:
                        one = jnp.dot(back[batch], w_hi, preferred_element_type=jnp.float32)
                        two = jnp.dot(back[batch, 0:tall], w_lo, preferred_element_type=jnp.float32)
                        change = one[:tall] + one[tall:] + two
                    perts[k] = perts[k] + change[:members]
                    means[k] = means[k] + change[members : members + 1]
            for k in range(len(xs)):
                x = means[k] + perts[k]
                for d in range(2):
                    start = (k % fields) * members * high + 2 * (together * q + k // fields) + d
                    lines[pl.ds(start, members, stride=high), :] = x[:, d * tcols : (d + 1) * tcols]
            return carry

        together = 2 if taken == third else 1
        lax.fori_loop(0, high // (2 * together), pairs, 0)

    most = jnp.maximum(active_ref[0], active_ref[1])

    @pl.when(most <= third)
    def _():
        run(third)

    @pl.when((most > third) & (most <= tcols))
    def _():
        run(tcols)

    @pl.when(most > tcols)
    def _():
        run(depth)


def on_device(n_lat, n_lon, ensemble, courant_cols, courant_rows, obs_value, obs_error, obs_cell, obs_kind, obs_live, obs_list):
    fields, members, trows, tcols = ensemble.shape
    slots = obs_value.shape[1]
    f32, i32 = jnp.float32, jnp.int32
    vmem = pl.BlockSpec(memory_space=pltpu.VMEM)
    smem = pl.BlockSpec(memory_space=pltpu.SMEM)
    lines = ensemble.reshape(fields * members * trows, tcols)
    raw = (lines, courant_cols, courant_rows, obs_value, obs_error, obs_live, obs_cell, jnp.transpose(obs_list, (2, 0, 1)))
    state, sides, tables = pl.pallas_call(
        functools.partial(exchange_kernel, (fields, members, trows, tcols, slots, n_lat, n_lon)),
        out_shape=(
            jax.ShapeDtypeStruct((fields * trows, members, tcols), f32),
            jax.ShapeDtypeStruct((2, members, tcols), f32),
            jax.ShapeDtypeStruct((2, 9, slots, tcols), f32),
        ),
        in_specs=[pl.BlockSpec(memory_space=pltpu.HBM)] * len(raw) + [smem, smem],
        out_specs=(pl.BlockSpec(memory_space=pltpu.HBM), vmem, vmem),
        scratch_shapes=[pltpu.VMEM((fields * trows, members, tcols), f32)] + [pltpu.VMEM(part.shape, part.dtype) for part in raw] + [
            pltpu.VMEM((2, EXTRA, tcols), f32),
            pltpu.VMEM((fields, trows + 2, members, tcols), f32),
            pltpu.VMEM((2, members, tcols), f32),
            pltpu.VMEM((2, members, tcols), f32),
            pltpu.VMEM((2, 9, slots, tcols), f32),
            pltpu.SemaphoreType.DMA((len(raw) - 1 + fields,)),
        ] + [pltpu.SemaphoreType.DMA((2,))] * 4 + [pltpu.SemaphoreType.DMA((2, 9))] * 2 + [pltpu.SemaphoreType.DMA],
        compiler_params=pltpu.CompilerParams(
            collective_id=0, has_side_effects=True, vmem_limit_bytes=64 * 2**20),
        name="exchange",
    )(*raw, obs_cell, obs_kind)

    high = 8
    depth = -(-9 * slots // 16) * 16
    tall = -(-(members + 1) // 16) * 16
    wide = -(-3 * members // tcols) * tcols
    return pl.pallas_call(
        functools.partial(update_kernel, (fields, members, trows, tcols, slots, high)),
        grid=(trows // high,),
        out_shape=jax.ShapeDtypeStruct(ensemble.shape, f32),
        in_specs=[
            pl.BlockSpec((fields, high, members, tcols), lambda i: (0, i, 0, 0)),
            pl.BlockSpec((2, members, tcols), lambda i: (0, 0, 0)),
            pl.BlockSpec((2, 9, slots, tcols), lambda i: (0, 0, 0, 0)),
        ],
        out_specs=pl.BlockSpec((fields, members, high, tcols), lambda i: (0, 0, i, 0)),
        scratch_shapes=[
            pltpu.VMEM((2, depth, wide), jnp.bfloat16),
            pltpu.VMEM((2, 2 * tall, depth), jnp.bfloat16),
            pltpu.VMEM((2, tall, 2 * tcols), jnp.bfloat16),
            pltpu.VMEM((2, 2 * tall, 2 * tcols), jnp.bfloat16),
            pltpu.VMEM((2, depth, tcols), f32),
            pltpu.VMEM((2, depth, tcols), f32),
            pltpu.SMEM((2,), i32),
        ],
        compiler_params=pltpu.CompilerParams(vmem_limit_bytes=64 * 2**20),
        name="update",
    )(state.reshape(fields, trows, members, tcols), sides, tables)


def solution(mesh):
    placed = (
        P(None, None, "lat", "lon"),
        P(None, "lat", "lon"),
        P(None, "lat", "lon"),
        P(None, ("lat", "lon")),
        P(None, ("lat", "lon")),
        P(None, ("lat", "lon")),
        P(None, ("lat", "lon")),
        P(None, ("lat", "lon")),
        P(None, ("lat", "lon"), None),
    )
    return jax.shard_map(
        functools.partial(on_device, mesh.shape["lat"], mesh.shape["lon"]),
        mesh=mesh,
        in_specs=placed,
        out_specs=P(None, None, "lat", "lon"),
        check_vma=False,
    )
```

```python
import functools
import jax
import jax.numpy as jnp
from jax import lax
from jax.sharding import PartitionSpec as P
from jax.experimental import pallas as pl
from jax.experimental.pallas import tpu as pltpu

MESH = pl.DeviceIdType.MESH
EXTRA = 16
HIGHEST = lax.Precision.HIGHEST
AROUND = [(a, b) for a in (-1, 0, 1) for b in (-1, 0, 1) if (a, b) != (0, 0)]


def slot_of(a, b):
    return (a + 1) * 3 + b + 1


def taper(dist):
    return jnp.square(jnp.maximum(0.0, 1.0 - jnp.abs(dist)))


def pad_rows(x, rows):
    if rows == x.shape[0]:
        return x
    return jnp.concatenate([x, jnp.zeros((rows - x.shape[0], x.shape[1]), x.dtype)], axis=0)


def table_columns(near, members, trows, tcols):
    rows, cols, factor = [], [], []
    for a in (-1, 0, 1):
        for b in (-1, 0, 1):
            block = near[slot_of(a, b)]
            rows.append(block[:, members + 3 : members + 4] + float(a * trows))
            cols.append(block[:, members + 4 : members + 5] + float(b * tcols))
            took = members + 5 + slot_of(-a, -b)
            factor.append(block[:, members + 1 : members + 2] * block[:, took : took + 1])
    return [jnp.concatenate(part, axis=0) for part in (rows, cols, factor)]


def make_table(prior, info):
    members, lanes = prior.shape
    ybar = jnp.sum(prior, axis=0, keepdims=True) / members
    yp = prior - ybar
    spread = jnp.sum(yp * yp, axis=0, keepdims=True) / (members - 1)
    value, live, error = info[0:1], info[1:2], info[2:3]
    total = spread + error
    gain = live / total
    alpha = 1.0 / (1.0 + jnp.sqrt(error / total))
    innov = value - ybar
    at = lax.broadcasted_iota(jnp.int32, info.shape, 0)
    extra = jnp.where(at == 0, innov, jnp.where(at == 1, gain, jnp.where(at == 2, alpha, info)))
    return jnp.transpose(pad_rows(jnp.concatenate([yp, extra], axis=0), lanes))


def exchange_kernel(
    sizes, x_hbm, cu_hbm, cv_hbm, value_hbm, error_hbm, live_hbm, cell_hbm, list_hbm, cell_ref, kind_ref,
    state_hbm, sides_ref, tables_ref,
    state_ref, x_ref, cu_ref, cv_ref, value_ref, error_ref, live_ref, cells_ref, list_ref, info,
    xt, pack, halo, near, in_sem, row_send, row_recv, col_send, col_recv, tab_send, tab_recv, out_sem,
):
    fields, members, trows, tcols, slots, n_lat, n_lon = sizes
    lat, lon = lax.axis_index("lat"), lax.axis_index("lon")

    def exists(a, b):
        r, c = lat + a, lon + b
        return (r >= 0) & (r < n_lat) & (c >= 0) & (c < n_lon)

    part = members * trows
    own_field = [pl.ds(f * part, part) for f in range(fields)]
    loads = [
        pltpu.make_async_copy(src, dst, in_sem.at[k])
        for k, (src, dst) in enumerate([(x_hbm.at[own], x_ref.at[own]) for own in own_field] + [
            (cu_hbm, cu_ref), (cv_hbm, cv_ref), (value_hbm, value_ref), (error_hbm, error_ref),
            (live_hbm, live_ref), (cell_hbm, cells_ref), (list_hbm, list_ref)])
    ]
    for copy in loads:
        copy.start()

    xt[:, 0] = jnp.zeros((fields, members, tcols), jnp.float32)
    xt[:, trows + 1] = jnp.zeros((fields, members, tcols), jnp.float32)
    halo[...] = jnp.zeros(halo.shape, jnp.float32)
    near[...] = jnp.zeros(near.shape, jnp.float32)
    info[...] = jnp.ones(info.shape, jnp.float32)

    barrier = pltpu.get_barrier_semaphore()
    for a, b in AROUND:
        @pl.when(exists(a, b))
        def _():
            pl.semaphore_signal(barrier, inc=1, device_id=(lat + a, lon + b), device_id_type=MESH)

    lane = lax.broadcasted_iota(jnp.int32, (members, tcols), 1)

    def turn(f, i, carry):
        west, east = carry
        tile = x_ref[pl.ds(f * part + i, members, stride=trows), :]
        xt[f, i + 1] = tile
        here = lane == f * trows + i
        west = jnp.where(here, jnp.broadcast_to(tile[:, 0:1], tile.shape), west)
        east = jnp.where(here, jnp.broadcast_to(tile[:, tcols - 1 : tcols], tile.shape), east)
        return west, east

    none = jnp.zeros((members, tcols), jnp.float32)
    west, east = none, none
    for f in range(fields):
        loads[f].wait()
        west, east = lax.fori_loop(0, trows, functools.partial(turn, f), (west, east), unroll=4)
    pack[0] = west
    pack[1] = east

    lat_n = jnp.where(lat > 0, 1, 0) + jnp.where(lat < n_lat - 1, 1, 0) + 1
    lon_n = jnp.where(lon > 0, 1, 0) + jnp.where(lon < n_lon - 1, 1, 0) + 1
    pl.semaphore_wait(barrier, lat_n * lon_n - 1)

    def row_copy(k):
        return pltpu.make_async_remote_copy(
            src_ref=xt.at[:, 1 if k == 0 else trows],
            dst_ref=xt.at[:, trows + 1 if k == 0 else 0],
            send_sem=row_send.at[k], recv_sem=row_recv.at[k],
            device_id=(lat - 1 if k == 0 else lat + 1, lon), device_id_type=MESH,
        )

    def col_copy(k):
        return pltpu.make_async_remote_copy(
            src_ref=pack.at[k], dst_ref=halo.at[k],
            send_sem=col_send.at[k], recv_sem=col_recv.at[k],
            device_id=(lat, lon - 1 if k == 0 else lon + 1), device_id_type=MESH,
        )

    for k, d in ((0, -1), (1, 1)):
        @pl.when(exists(0, d))
        def _():
            col_copy(k).start()

        @pl.when(exists(d, 0))
        def _():
            row_copy(k).start()

    for copy in loads[fields:]:
        copy.wait()

    edge = lax.broadcasted_iota(jnp.int32, (8, tcols), 1)

    def advect(i, carry):
        u = jnp.broadcast_to(cu_ref[0, pl.ds(i, 1), :], (8, tcols))
        v = jnp.broadcast_to(cv_ref[0, pl.ds(i, 1), :], (8, tcols))
        hu, hv = 0.5 * u, 0.5 * v
        huu, hvv = hu * u, hv * v
        all_of = lambda c: jnp.concatenate([c] * (members // 8), axis=0)
        c_mid = all_of(1.0 - 2.0 * (huu + hvv))
        c_east = all_of(jnp.where(edge == tcols - 1, 0.0, huu - hu))
        c_west = all_of(jnp.where(edge == 0, 0.0, huu + hu))
        c_north, c_south = all_of(hvv - hv), all_of(hvv + hv)
        for f in range(fields):
            mid = xt[f, i + 1]
            across = c_east * pltpu.roll(mid, tcols - 1, 1) + c_west * pltpu.roll(mid, 1, 1)
            state_ref[f * trows + i] = c_mid * mid + across + (c_north * xt[f, i + 2] + c_south * xt[f, i])
        return carry

    lax.fori_loop(1, trows - 1, advect, 0, unroll=2)

    for batch in range(2):
        own = pl.ds(0, slots)
        cells = cells_ref[batch : batch + 1, :]
        info[batch, 0:1, own] = value_ref[batch : batch + 1, :]
        info[batch, 1:2, own] = live_ref[batch : batch + 1, :].astype(jnp.float32)
        info[batch, 2:3, own] = error_ref[batch : batch + 1, :]
        row = jnp.floor((cells.astype(jnp.float32) + 0.5) * (1.0 / tcols))
        info[batch, 3:4, own] = row
        info[batch, 4:5, own] = cells.astype(jnp.float32) - row * tcols
        for k in range(list_ref.shape[0]):
            info[batch, 5 + k : 6 + k, own] = list_ref[k, batch : batch + 1, :].astype(jnp.float32)

    def along(column):
        spread = jnp.broadcast_to(column, (trows, tcols))
        line = jnp.transpose(pad_rows(spread, tcols))[0:1]
        total = line
        for f in range(1, fields):
            total = total + pltpu.roll(jnp.broadcast_to(line, (8, tcols)), f * trows, 1)[0:1]
        return total

    u = cu_ref[0]
    rise = along((0.5 * u + 0.5 * u * u)[:, 0:1])
    fall = along((0.5 * u * u - 0.5 * u)[:, tcols - 1 : tcols])

    for k, d in ((0, -1), (1, 1)):
        @pl.when(exists(0, d))
        def _():
            col_copy(k).wait_send()

        @pl.when(exists(d, 0))
        def _():
            row_copy(k).wait_send()

        @pl.when(exists(0, -d))
        def _():
            col_copy(k).wait_recv()

        @pl.when(exists(-d, 0))
        def _():
            row_copy(k).wait_recv()

    advect(0, 0)
    advect(trows - 1, 0)
    keep = pltpu.make_async_copy(state_ref, state_hbm, out_sem)
    keep.start()
    first_add = halo[1] * rise
    last_add = halo[0] * fall
    sides_ref[0] = first_add
    sides_ref[1] = last_add

    def gather(batch):
        prior = none
        for s in range(slots):
            cell = cell_ref[batch, s]
            col = lax.rem(cell, tcols)
            at = kind_ref[batch, s] * trows + lax.div(cell, tcols)
            tile = state_ref[at]
            here = lane == at
            picked = jnp.where(lane == col, tile, 0.0)
            picked = picked + jnp.where(here & (col == 0), first_add, 0.0)
            picked = picked + jnp.where(here & (col == tcols - 1), last_add, 0.0)
            column = jnp.sum(picked, axis=1, keepdims=True)
            prior = jnp.where(lane == s, jnp.broadcast_to(column, tile.shape), prior)
        return prior

    def table_copy(batch, a, b):
        return pltpu.make_async_remote_copy(
            src_ref=near.at[batch, slot_of(0, 0)],
            dst_ref=near.at[batch, slot_of(-a, -b)],
            send_sem=tab_send.at[batch, slot_of(a, b)],
            recv_sem=tab_recv.at[batch, slot_of(-a, -b)],
            device_id=(lat + a, lon + b), device_id_type=MESH,
        )

    def send(batch, prior):
        near[batch, slot_of(0, 0)] = make_table(prior, info[batch])[:slots]
        for a, b in AROUND:
            @pl.when(exists(a, b))
            def _():
                table_copy(batch, a, b).start()

    def finish(batch):
        for a, b in AROUND:
            @pl.when(exists(a, b))
            def _():
                table_copy(batch, a, b).wait_send()

            @pl.when(exists(-a, -b))
            def _():
                table_copy(batch, a, b).wait_recv()

    send(0, gather(0))
    later = gather(1)
    finish(0)

    board = [near[0, k] for k in range(9)]
    rows, cols, factor = table_columns(board, members, trows, tcols)
    whole = jnp.concatenate(board, axis=0)
    count = whole.shape[0]
    loc = taper((rows - info[1, 3:4]) / trows) * factor * taper((cols - info[1, 4:5]) / trows)
    mean = jnp.sum(later, axis=0, keepdims=True) / members
    pert = later - mean
    shut = lax.broadcasted_iota(jnp.int32, whole.shape, 1)
    yp = jnp.where(shut < members, whole, 0.0)
    proj = jnp.dot(yp, pad_rows(pert, tcols), precision=HIGHEST, preferred_element_type=jnp.float32)
    weight = proj * loc * (1.0 / (members - 1))
    mean = mean + jnp.sum(weight * whole[:, members : members + 1], axis=0, keepdims=True)
    scaled = whole * whole[:, members + 2 : members + 3]
    full = -(-count // tcols) * tcols
    change = jnp.dot(
        jnp.transpose(pad_rows(scaled, full))[:members], pad_rows(weight, full),
        precision=HIGHEST, preferred_element_type=jnp.float32,
    )
    send(1, mean + pert - change)
    finish(1)
    tables_ref[...] = near[...]
    keep.wait()


def split(x):
    hi = x.astype(jnp.bfloat16)
    return hi, (x - hi.astype(jnp.float32)).astype(jnp.bfloat16)


def beside(parts, rows, lanes):
    width = parts[0][1]
    total = [jnp.zeros((rows, lanes), jnp.float32) for _ in range(2)]
    at = lax.broadcasted_iota(jnp.int32, (rows, lanes), 1)
    for k, (part, _) in enumerate(parts):
        start = k * width
        turned = pltpu.roll(part, start % lanes, 1) if start % lanes else part
        for block in range(2):
            lower, upper = start - block * lanes, start + width - block * lanes
            if upper > 0 and lower < lanes:
                total[block] = jnp.where((at >= lower) & (at < upper), turned, total[block])
    return jnp.concatenate(total, axis=1)


def update_kernel(sizes, state_ref, sides_ref, tables_ref, out_ref, left, back, back3, back2, rowrel, colw, active_ref):
    fields, members, trows, tcols, slots, high = sizes
    depth = left.shape[1]
    wide = left.shape[2]
    tall = back.shape[1] // 2
    third = 2 * tcols // 48 * 16
    step = pl.program_id(0)

    @pl.when(step == 0)
    def _():
        for batch in range(2):
            board = [tables_ref[batch, k] for k in range(9)]
            rows, cols, factor = table_columns(board, members, trows, tcols)
            whole = jnp.concatenate(board, axis=0)
            lane = lax.broadcasted_iota(jnp.int32, whole.shape, 1)
            reach = (
                (factor != 0.0) & (rows > -trows) & (rows < 2 * trows - 1)
                & (cols > -trows) & (cols < tcols - 1 + trows)
            )
            active = jnp.where(reach, 1.0, 0.0)
            whole = jnp.where(lane == members + 1, factor * (1.0 / (members - 1)), whole)
            whole = jnp.where(lane == members + 3, rows, whole)
            whole = jnp.where(lane == members + 4, cols, whole)
            whole = jnp.where(lane == members + 5, active, whole)
            full = -(-depth // tcols) * tcols
            whole = pad_rows(whole, full)
            flags = jnp.transpose(whole)[members + 5 : members + 6]
            r = lax.broadcasted_iota(jnp.int32, (full, full), 0)
            c = lax.broadcasted_iota(jnp.int32, (full, full), 1)
            upper = jnp.where(r <= c, 1.0, 0.0).astype(jnp.bfloat16)
            line = jnp.broadcast_to(flags, (16, full)).astype(jnp.bfloat16)
            running = jnp.dot(line, upper, preferred_element_type=jnp.float32)[0:1]
            active_ref[batch] = jnp.max(running).astype(jnp.int32)
            pick = jnp.where((running - 1.0 == r.astype(jnp.float32)) & (flags > 0.5), 1.0, 0.0)
            whole = jnp.dot(pick, whole, precision=HIGHEST, preferred_element_type=jnp.float32)

            lane = lax.broadcasted_iota(jnp.int32, whole.shape, 1)
            yp = jnp.where(lane < members, whole, 0.0)
            hi = yp.astype(jnp.bfloat16).astype(jnp.float32)
            lo = yp - hi
            both = beside([(hi, members), (lo, members), (hi, members)], full, tcols)
            left[batch] = both[:depth].astype(jnp.bfloat16)
            turned = jnp.transpose(whole)
            alpha = turned[members + 2 : members + 3]
            turned = turned[:tall]
            at = lax.broadcasted_iota(jnp.int32, turned.shape, 0)
            scaled = jnp.where(at < members, -alpha * turned, jnp.where(at == members, turned, 0.0))
            hi, lo = split(scaled)
            back[batch, 0:tall] = hi[:, :depth]
            back[batch, tall:] = lo[:, :depth]
            hi = hi.astype(jnp.float32)[:, :tcols]
            lo = lo.astype(jnp.float32)[:, :tcols]
            back3[batch] = beside([(hi, third), (lo, third), (hi, third)], tall, tcols).astype(jnp.bfloat16)
            back2[batch, 0:tall] = jnp.concatenate([hi, hi], axis=1).astype(jnp.bfloat16)
            back2[batch, tall:] = jnp.concatenate([lo, jnp.zeros_like(lo)], axis=1).astype(jnp.bfloat16)
            column = lane.astype(jnp.float32)
            near_w = taper((whole[:, members + 4 : members + 5] - column) / trows) * whole[:, members + 1 : members + 2]
            colw[batch] = near_w[:depth]
            rowrel[batch] = jnp.broadcast_to(whole[:, members + 3 : members + 4], whole.shape)[:depth]

    lines = out_ref.reshape(fields * members * high, tcols)
    lane = lax.broadcasted_iota(jnp.int32, (members, tcols), 1)

    def run(taken):
        def zero_rows(rows):
            return [jnp.zeros((rows, 2 * tcols), jnp.bfloat16)] if rows else []

        def pairs(q, carry):
            locs, xs = [], []
            for p in range(together):
                row = step * high + 2 * (together * q + p)
                locs.append([])
                for batch in range(2):
                    parts = []
                    for d in range(2):
                        z = (rowrel[batch, 0:taken] - (row + d).astype(jnp.float32)) * (1.0 / trows)
                        parts.append(taper(z) * colw[batch, 0:taken])
                    locs[p].append(jnp.concatenate(parts, axis=1))
                for f in range(fields):
                    tiles = []
                    for d in range(2):
                        at = f * trows + row + d
                        first = pltpu.roll(sides_ref[0], lax.rem(tcols - at, tcols), 1)
                        last = pltpu.roll(sides_ref[1], tcols - 1 - at, 1)
                        add = jnp.where(lane == 0, first, jnp.where(lane == tcols - 1, last, 0.0))
                        tiles.append(state_ref[f, 2 * (together * q + p) + d] + add)
                    xs.append(jnp.concatenate(tiles, axis=1))
            means = [jnp.sum(x, axis=0, keepdims=True) * (1.0 / members) for x in xs]
            perts = [x - mean for x, mean in zip(xs, means)]
            for batch in range(2):
                projs = []
                for k in range(len(xs)):
                    hi, lo = split(perts[k])
                    right = jnp.concatenate([hi, hi, lo] + zero_rows(wide - 3 * members), axis=0)
                    projs.append(jnp.dot(left[batch, 0:taken], right, preferred_element_type=jnp.float32))
                for k in range(len(xs)):
                    w_hi, w_lo = split(projs[k] * locs[k // fields][batch])
                    if taken == third:
                        stack = jnp.concatenate([w_hi, w_hi, w_lo] + zero_rows(2 * tcols - 3 * third), axis=0)
                        change = jnp.dot(back3[batch], stack, preferred_element_type=jnp.float32)
                    elif taken == tcols:
                        stack = jnp.concatenate([w_hi, w_lo], axis=0)
                        one = jnp.dot(back2[batch], stack, preferred_element_type=jnp.float32)
                        change = one[:tall] + one[tall:]
                    else:
                        one = jnp.dot(back[batch], w_hi, preferred_element_type=jnp.float32)
                        two = jnp.dot(back[batch, 0:tall], w_lo, preferred_element_type=jnp.float32)
                        change = one[:tall] + one[tall:] + two
                    perts[k] = perts[k] + change[:members]
                    means[k] = means[k] + change[members : members + 1]
            for k in range(len(xs)):
                x = means[k] + perts[k]
                for d in range(2):
                    start = (k % fields) * members * high + 2 * (together * q + k // fields) + d
                    lines[pl.ds(start, members, stride=high), :] = x[:, d * tcols : (d + 1) * tcols]
            return carry

        together = high // 2 if taken == third else 1
        lax.fori_loop(0, high // (2 * together), pairs, 0)

    most = jnp.maximum(active_ref[0], active_ref[1])

    @pl.when(most <= third)
    def _():
        run(third)

    @pl.when((most > third) & (most <= tcols))
    def _():
        run(tcols)

    @pl.when(most > tcols)
    def _():
        run(depth)


def on_device(n_lat, n_lon, ensemble, courant_cols, courant_rows, obs_value, obs_error, obs_cell, obs_kind, obs_live, obs_list):
    fields, members, trows, tcols = ensemble.shape
    slots = obs_value.shape[1]
    f32, i32 = jnp.float32, jnp.int32
    vmem = pl.BlockSpec(memory_space=pltpu.VMEM)
    smem = pl.BlockSpec(memory_space=pltpu.SMEM)
    lines = ensemble.reshape(fields * members * trows, tcols)
    raw = (lines, courant_cols, courant_rows, obs_value, obs_error, obs_live, obs_cell, jnp.transpose(obs_list, (2, 0, 1)))
    state, sides, tables = pl.pallas_call(
        functools.partial(exchange_kernel, (fields, members, trows, tcols, slots, n_lat, n_lon)),
        out_shape=(
            jax.ShapeDtypeStruct((fields * trows, members, tcols), f32),
            jax.ShapeDtypeStruct((2, members, tcols), f32),
            jax.ShapeDtypeStruct((2, 9, slots, tcols), f32),
        ),
        in_specs=[pl.BlockSpec(memory_space=pltpu.HBM)] * len(raw) + [smem, smem],
        out_specs=(pl.BlockSpec(memory_space=pltpu.HBM), vmem, vmem),
        scratch_shapes=[pltpu.VMEM((fields * trows, members, tcols), f32)] + [pltpu.VMEM(part.shape, part.dtype) for part in raw] + [
            pltpu.VMEM((2, EXTRA, tcols), f32),
            pltpu.VMEM((fields, trows + 2, members, tcols), f32),
            pltpu.VMEM((2, members, tcols), f32),
            pltpu.VMEM((2, members, tcols), f32),
            pltpu.VMEM((2, 9, slots, tcols), f32),
            pltpu.SemaphoreType.DMA((len(raw) - 1 + fields,)),
        ] + [pltpu.SemaphoreType.DMA((2,))] * 4 + [pltpu.SemaphoreType.DMA((2, 9))] * 2 + [pltpu.SemaphoreType.DMA],
        compiler_params=pltpu.CompilerParams(
            collective_id=0, has_side_effects=True, vmem_limit_bytes=64 * 2**20),
        name="exchange",
    )(*raw, obs_cell, obs_kind)

    high = 8
    depth = -(-9 * slots // 16) * 16
    tall = -(-(members + 1) // 16) * 16
    wide = -(-3 * members // tcols) * tcols
    return pl.pallas_call(
        functools.partial(update_kernel, (fields, members, trows, tcols, slots, high)),
        grid=(trows // high,),
        out_shape=jax.ShapeDtypeStruct(ensemble.shape, f32),
        in_specs=[
            pl.BlockSpec((fields, high, members, tcols), lambda i: (0, i, 0, 0)),
            pl.BlockSpec((2, members, tcols), lambda i: (0, 0, 0)),
            pl.BlockSpec((2, 9, slots, tcols), lambda i: (0, 0, 0, 0)),
        ],
        out_specs=pl.BlockSpec((fields, members, high, tcols), lambda i: (0, 0, i, 0)),
        scratch_shapes=[
            pltpu.VMEM((2, depth, wide), jnp.bfloat16),
            pltpu.VMEM((2, 2 * tall, depth), jnp.bfloat16),
            pltpu.VMEM((2, tall, 2 * tcols), jnp.bfloat16),
            pltpu.VMEM((2, 2 * tall, 2 * tcols), jnp.bfloat16),
            pltpu.VMEM((2, depth, tcols), f32),
            pltpu.VMEM((2, depth, tcols), f32),
            pltpu.SMEM((2,), i32),
        ],
        compiler_params=pltpu.CompilerParams(vmem_limit_bytes=64 * 2**20),
        name="update",
    )(state.reshape(fields, trows, members, tcols), sides, tables)


def solution(mesh):
    placed = (
        P(None, None, "lat", "lon"),
        P(None, "lat", "lon"),
        P(None, "lat", "lon"),
        P(None, ("lat", "lon")),
        P(None, ("lat", "lon")),
        P(None, ("lat", "lon")),
        P(None, ("lat", "lon")),
        P(None, ("lat", "lon")),
        P(None, ("lat", "lon"), None),
    )
    return jax.shard_map(
        functools.partial(on_device, mesh.shape["lat"], mesh.shape["lon"]),
        mesh=mesh,
        in_specs=placed,
        out_specs=P(None, None, "lat", "lon"),
        check_vma=False,
    )
```

```python
import functools
import jax
import jax.numpy as jnp
from jax import lax
from jax.sharding import PartitionSpec as P
from jax.experimental import pallas as pl
from jax.experimental.pallas import tpu as pltpu

MESH = pl.DeviceIdType.MESH
EXTRA = 16
HIGHEST = lax.Precision.HIGHEST
AROUND = [(a, b) for a in (-1, 0, 1) for b in (-1, 0, 1) if (a, b) != (0, 0)]


def slot_of(a, b):
    return (a + 1) * 3 + b + 1


def taper(dist):
    return jnp.square(jnp.maximum(0.0, 1.0 - jnp.abs(dist)))


def pad_rows(x, rows):
    if rows == x.shape[0]:
        return x
    return jnp.concatenate([x, jnp.zeros((rows - x.shape[0], x.shape[1]), x.dtype)], axis=0)


def table_columns(near, members, trows, tcols):
    rows, cols, factor = [], [], []
    for a in (-1, 0, 1):
        for b in (-1, 0, 1):
            block = near[slot_of(a, b)]
            rows.append(block[:, members + 3 : members + 4] + float(a * trows))
            cols.append(block[:, members + 4 : members + 5] + float(b * tcols))
            took = members + 5 + slot_of(-a, -b)
            factor.append(block[:, members + 1 : members + 2] * block[:, took : took + 1])
    return [jnp.concatenate(part, axis=0) for part in (rows, cols, factor)]


def make_table(prior, info):
    members, lanes = prior.shape
    ybar = jnp.sum(prior, axis=0, keepdims=True) / members
    yp = prior - ybar
    spread = jnp.sum(yp * yp, axis=0, keepdims=True) / (members - 1)
    value, live, error = info[0:1], info[1:2], info[2:3]
    total = spread + error
    gain = live / total
    alpha = 1.0 / (1.0 + jnp.sqrt(error / total))
    innov = value - ybar
    at = lax.broadcasted_iota(jnp.int32, info.shape, 0)
    extra = jnp.where(at == 0, innov, jnp.where(at == 1, gain, jnp.where(at == 2, alpha, info)))
    return jnp.transpose(pad_rows(jnp.concatenate([yp, extra], axis=0), lanes))


def exchange_kernel(
    sizes, x_hbm, cu_hbm, cv_hbm, value_hbm, error_hbm, live_hbm, cell_hbm, list_hbm, cell_ref, kind_ref,
    state_hbm, sides_ref, tables_ref,
    state_ref, x_ref, cu_ref, cv_ref, value_ref, error_ref, live_ref, cells_ref, list_ref, info,
    xt, pack, halo, near, in_sem, row_send, row_recv, col_send, col_recv, tab_send, tab_recv, out_sem,
):
    fields, members, trows, tcols, slots, n_lat, n_lon = sizes
    lat, lon = lax.axis_index("lat"), lax.axis_index("lon")

    def exists(a, b):
        r, c = lat + a, lon + b
        return (r >= 0) & (r < n_lat) & (c >= 0) & (c < n_lon)

    part = members * trows
    own_field = [pl.ds(f * part, part) for f in range(fields)]
    loads = [
        pltpu.make_async_copy(src, dst, in_sem.at[k])
        for k, (src, dst) in enumerate([(x_hbm.at[own], x_ref.at[own]) for own in own_field] + [
            (cu_hbm, cu_ref), (cv_hbm, cv_ref), (value_hbm, value_ref), (error_hbm, error_ref),
            (live_hbm, live_ref), (cell_hbm, cells_ref), (list_hbm, list_ref)])
    ]
    for copy in loads:
        copy.start()

    xt[:, 0] = jnp.zeros((fields, members, tcols), jnp.float32)
    xt[:, trows + 1] = jnp.zeros((fields, members, tcols), jnp.float32)
    halo[...] = jnp.zeros(halo.shape, jnp.float32)
    near[...] = jnp.zeros(near.shape, jnp.float32)
    info[...] = jnp.ones(info.shape, jnp.float32)

    barrier = pltpu.get_barrier_semaphore()
    for a, b in AROUND:
        @pl.when(exists(a, b))
        def _():
            pl.semaphore_signal(barrier, inc=1, device_id=(lat + a, lon + b), device_id_type=MESH)

    lane = lax.broadcasted_iota(jnp.int32, (members, tcols), 1)

    def turn(f, i, carry):
        west, east = carry
        tile = x_ref[pl.ds(f * part + i, members, stride=trows), :]
        xt[f, i + 1] = tile
        here = lane == f * trows + i
        west = jnp.where(here, jnp.broadcast_to(tile[:, 0:1], tile.shape), west)
        east = jnp.where(here, jnp.broadcast_to(tile[:, tcols - 1 : tcols], tile.shape), east)
        return west, east

    none = jnp.zeros((members, tcols), jnp.float32)
    west, east = none, none
    for f in range(fields):
        loads[f].wait()
        west, east = lax.fori_loop(0, trows, functools.partial(turn, f), (west, east), unroll=4)
    pack[0] = west
    pack[1] = east

    lat_n = jnp.where(lat > 0, 1, 0) + jnp.where(lat < n_lat - 1, 1, 0) + 1
    lon_n = jnp.where(lon > 0, 1, 0) + jnp.where(lon < n_lon - 1, 1, 0) + 1
    pl.semaphore_wait(barrier, lat_n * lon_n - 1)

    def row_copy(k):
        return pltpu.make_async_remote_copy(
            src_ref=xt.at[:, 1 if k == 0 else trows],
            dst_ref=xt.at[:, trows + 1 if k == 0 else 0],
            send_sem=row_send.at[k], recv_sem=row_recv.at[k],
            device_id=(lat - 1 if k == 0 else lat + 1, lon), device_id_type=MESH,
        )

    def col_copy(k):
        return pltpu.make_async_remote_copy(
            src_ref=pack.at[k], dst_ref=halo.at[k],
            send_sem=col_send.at[k], recv_sem=col_recv.at[k],
            device_id=(lat, lon - 1 if k == 0 else lon + 1), device_id_type=MESH,
        )

    for k, d in ((0, -1), (1, 1)):
        @pl.when(exists(0, d))
        def _():
            col_copy(k).start()

        @pl.when(exists(d, 0))
        def _():
            row_copy(k).start()

    for copy in loads[fields:]:
        copy.wait()

    edge = lax.broadcasted_iota(jnp.int32, (8, tcols), 1)

    def advect(i, carry):
        u = jnp.broadcast_to(cu_ref[0, pl.ds(i, 1), :], (8, tcols))
        v = jnp.broadcast_to(cv_ref[0, pl.ds(i, 1), :], (8, tcols))
        hu, hv = 0.5 * u, 0.5 * v
        huu, hvv = hu * u, hv * v
        all_of = lambda c: jnp.concatenate([c] * (members // 8), axis=0)
        c_mid = all_of(1.0 - 2.0 * (huu + hvv))
        c_east = all_of(jnp.where(edge == tcols - 1, 0.0, huu - hu))
        c_west = all_of(jnp.where(edge == 0, 0.0, huu + hu))
        c_north, c_south = all_of(hvv - hv), all_of(hvv + hv)
        for f in range(fields):
            mid = xt[f, i + 1]
            across = c_east * pltpu.roll(mid, tcols - 1, 1) + c_west * pltpu.roll(mid, 1, 1)
            state_ref[f * trows + i] = c_mid * mid + across + (c_north * xt[f, i + 2] + c_south * xt[f, i])
        return carry

    lax.fori_loop(1, trows - 1, advect, 0, unroll=2)

    for batch in range(2):
        own = pl.ds(0, slots)
        cells = cells_ref[batch : batch + 1, :]
        info[batch, 0:1, own] = value_ref[batch : batch + 1, :]
        info[batch, 1:2, own] = live_ref[batch : batch + 1, :].astype(jnp.float32)
        info[batch, 2:3, own] = error_ref[batch : batch + 1, :]
        row = jnp.floor((cells.astype(jnp.float32) + 0.5) * (1.0 / tcols))
        info[batch, 3:4, own] = row
        info[batch, 4:5, own] = cells.astype(jnp.float32) - row * tcols
        for k in range(list_ref.shape[0]):
            info[batch, 5 + k : 6 + k, own] = list_ref[k, batch : batch + 1, :].astype(jnp.float32)

    def along(column):
        spread = jnp.broadcast_to(column, (trows, tcols))
        line = jnp.transpose(pad_rows(spread, tcols))[0:1]
        total = line
        for f in range(1, fields):
            total = total + pltpu.roll(jnp.broadcast_to(line, (8, tcols)), f * trows, 1)[0:1]
        return total

    u = cu_ref[0]
    rise = along((0.5 * u + 0.5 * u * u)[:, 0:1])
    fall = along((0.5 * u * u - 0.5 * u)[:, tcols - 1 : tcols])

    for k, d in ((0, -1), (1, 1)):
        @pl.when(exists(0, d))
        def _():
            col_copy(k).wait_send()

        @pl.when(exists(d, 0))
        def _():
            row_copy(k).wait_send()

        @pl.when(exists(0, -d))
        def _():
            col_copy(k).wait_recv()

        @pl.when(exists(-d, 0))
        def _():
            row_copy(k).wait_recv()

    advect(0, 0)
    advect(trows - 1, 0)
    keep = pltpu.make_async_copy(state_ref, state_hbm, out_sem)
    keep.start()
    first_add = halo[1] * rise
    last_add = halo[0] * fall
    sides_ref[0] = first_add
    sides_ref[1] = last_add

    def gather(batch):
        prior = none
        for s in range(slots):
            cell = cell_ref[batch, s]
            col = lax.rem(cell, tcols)
            at = kind_ref[batch, s] * trows + lax.div(cell, tcols)
            tile = state_ref[at]
            here = lane == at
            picked = jnp.where(lane == col, tile, 0.0)
            picked = picked + jnp.where(here & (col == 0), first_add, 0.0)
            picked = picked + jnp.where(here & (col == tcols - 1), last_add, 0.0)
            column = jnp.sum(picked, axis=1, keepdims=True)
            prior = jnp.where(lane == s, jnp.broadcast_to(column, tile.shape), prior)
        return prior

    def table_copy(batch, a, b):
        return pltpu.make_async_remote_copy(
            src_ref=near.at[batch, slot_of(0, 0)],
            dst_ref=near.at[batch, slot_of(-a, -b)],
            send_sem=tab_send.at[batch, slot_of(a, b)],
            recv_sem=tab_recv.at[batch, slot_of(-a, -b)],
            device_id=(lat + a, lon + b), device_id_type=MESH,
        )

    def send(batch, prior):
        near[batch, slot_of(0, 0)] = make_table(prior, info[batch])[:slots]
        for a, b in AROUND:
            @pl.when(exists(a, b))
            def _():
                table_copy(batch, a, b).start()

    def finish(batch):
        for a, b in AROUND:
            @pl.when(exists(a, b))
            def _():
                table_copy(batch, a, b).wait_send()

            @pl.when(exists(-a, -b))
            def _():
                table_copy(batch, a, b).wait_recv()

    send(0, gather(0))
    later = gather(1)
    finish(0)

    board = [near[0, k] for k in range(9)]
    rows, cols, factor = table_columns(board, members, trows, tcols)
    whole = jnp.concatenate(board, axis=0)
    count = whole.shape[0]
    loc = taper((rows - info[1, 3:4]) / trows) * factor * taper((cols - info[1, 4:5]) / trows)
    mean = jnp.sum(later, axis=0, keepdims=True) / members
    pert = later - mean
    shut = lax.broadcasted_iota(jnp.int32, whole.shape, 1)
    yp = jnp.where(shut < members, whole, 0.0)
    proj = jnp.dot(yp, pad_rows(pert, tcols), precision=HIGHEST, preferred_element_type=jnp.float32)
    weight = proj * loc * (1.0 / (members - 1))
    mean = mean + jnp.sum(weight * whole[:, members : members + 1], axis=0, keepdims=True)
    scaled = whole * whole[:, members + 2 : members + 3]
    full = -(-count // tcols) * tcols
    change = jnp.dot(
        jnp.transpose(pad_rows(scaled, full))[:members], pad_rows(weight, full),
        precision=HIGHEST, preferred_element_type=jnp.float32,
    )
    send(1, mean + pert - change)
    finish(1)
    tables_ref[...] = near[...]
    keep.wait()


def split(x):
    hi = x.astype(jnp.bfloat16)
    return hi, (x - hi.astype(jnp.float32)).astype(jnp.bfloat16)


def beside(parts, rows, lanes):
    width = parts[0][1]
    total = [jnp.zeros((rows, lanes), jnp.float32) for _ in range(2)]
    at = lax.broadcasted_iota(jnp.int32, (rows, lanes), 1)
    for k, (part, _) in enumerate(parts):
        start = k * width
        turned = pltpu.roll(part, start % lanes, 1) if start % lanes else part
        for block in range(2):
            lower, upper = start - block * lanes, start + width - block * lanes
            if upper > 0 and lower < lanes:
                total[block] = jnp.where((at >= lower) & (at < upper), turned, total[block])
    return jnp.concatenate(total, axis=1)


def update_kernel(sizes, state_ref, sides_ref, tables_ref, out_ref, left, back, back3, back2, rowrel, colw, active_ref):
    fields, members, trows, tcols, slots, high = sizes
    depth = left.shape[1]
    wide = left.shape[2]
    tall = back.shape[1] // 2
    third = 2 * tcols // 48 * 16
    step = pl.program_id(0)

    @pl.when(step == 0)
    def _():
        for batch in range(2):
            board = [tables_ref[batch, k] for k in range(9)]
            rows, cols, factor = table_columns(board, members, trows, tcols)
            whole = jnp.concatenate(board, axis=0)
            lane = lax.broadcasted_iota(jnp.int32, whole.shape, 1)
            reach = (
                (factor != 0.0) & (rows > -trows) & (rows < 2 * trows - 1)
                & (cols > -trows) & (cols < tcols - 1 + trows)
            )
            active = jnp.where(reach, 1.0, 0.0)
            whole = jnp.where(lane == members + 1, factor * (1.0 / (members - 1)), whole)
            whole = jnp.where(lane == members + 3, rows, whole)
            whole = jnp.where(lane == members + 4, cols, whole)
            whole = jnp.where(lane == members + 5, active, whole)
            full = -(-depth // tcols) * tcols
            whole = pad_rows(whole, full)
            flags = jnp.transpose(whole)[members + 5 : members + 6]
            r = lax.broadcasted_iota(jnp.int32, (full, full), 0)
            c = lax.broadcasted_iota(jnp.int32, (full, full), 1)
            upper = jnp.where(r <= c, 1.0, 0.0).astype(jnp.bfloat16)
            line = jnp.broadcast_to(flags, (16, full)).astype(jnp.bfloat16)
            running = jnp.dot(line, upper, preferred_element_type=jnp.float32)[0:1]
            active_ref[batch] = jnp.max(running).astype(jnp.int32)
            pick = jnp.where((running - 1.0 == r.astype(jnp.float32)) & (flags > 0.5), 1.0, 0.0)
            pick = pick.astype(jnp.bfloat16)
            top, rest = whole.astype(jnp.bfloat16), whole
            rest = rest - top.astype(jnp.float32)
            middle, last = split(rest)
            picked = jnp.dot(pick, jnp.concatenate([top, middle], axis=1), preferred_element_type=jnp.float32)
            whole = picked[:, :tcols] + picked[:, tcols:] + jnp.dot(pick, last, preferred_element_type=jnp.float32)

            lane = lax.broadcasted_iota(jnp.int32, whole.shape, 1)
            yp = jnp.where(lane < members, whole, 0.0)
            hi = yp.astype(jnp.bfloat16).astype(jnp.float32)
            lo = yp - hi
            both = beside([(hi, members), (lo, members), (hi, members)], full, tcols)
            left[batch] = both[:depth].astype(jnp.bfloat16)
            turned = jnp.transpose(whole)
            alpha = turned[members + 2 : members + 3]
            turned = turned[:tall]
            at = lax.broadcasted_iota(jnp.int32, turned.shape, 0)
            scaled = jnp.where(at < members, -alpha * turned, jnp.where(at == members, turned, 0.0))
            hi, lo = split(scaled)
            back[batch, 0:tall] = hi[:, :depth]
            back[batch, tall:] = lo[:, :depth]
            hi = hi.astype(jnp.float32)[:, :tcols]
            lo = lo.astype(jnp.float32)[:, :tcols]
            back3[batch] = beside([(hi, third), (lo, third), (hi, third)], tall, tcols).astype(jnp.bfloat16)
            back2[batch, 0:tall] = jnp.concatenate([hi, hi], axis=1).astype(jnp.bfloat16)
            back2[batch, tall:] = jnp.concatenate([lo, jnp.zeros_like(lo)], axis=1).astype(jnp.bfloat16)
            column = lane.astype(jnp.float32)
            near_w = taper((whole[:, members + 4 : members + 5] - column) / trows) * whole[:, members + 1 : members + 2]
            colw[batch] = near_w[:depth]
            rowrel[batch] = jnp.broadcast_to(whole[:, members + 3 : members + 4], whole.shape)[:depth]

    lines = out_ref.reshape(fields * members * high, tcols)
    lane = lax.broadcasted_iota(jnp.int32, (members, tcols), 1)

    def run(taken):
        def zero_rows(rows):
            return [jnp.zeros((rows, 2 * tcols), jnp.bfloat16)] if rows else []

        def pairs(q, carry):
            locs, xs = [], []
            for p in range(together):
                row = step * high + 2 * (together * q + p)
                locs.append([])
                for batch in range(2):
                    parts = []
                    for d in range(2):
                        z = (rowrel[batch, 0:taken] - (row + d).astype(jnp.float32)) * (1.0 / trows)
                        parts.append(taper(z) * colw[batch, 0:taken])
                    locs[p].append(jnp.concatenate(parts, axis=1))
                for f in range(fields):
                    tiles = []
                    for d in range(2):
                        at = f * trows + row + d
                        first = pltpu.roll(sides_ref[0], lax.rem(tcols - at, tcols), 1)
                        last = pltpu.roll(sides_ref[1], tcols - 1 - at, 1)
                        add = jnp.where(lane == 0, first, jnp.where(lane == tcols - 1, last, 0.0))
                        tiles.append(state_ref[f, 2 * (together * q + p) + d] + add)
                    xs.append(jnp.concatenate(tiles, axis=1))
            means = [jnp.sum(x, axis=0, keepdims=True) * (1.0 / members) for x in xs]
            perts = [x - mean for x, mean in zip(xs, means)]
            for batch in range(2):
                projs = []
                for k in range(len(xs)):
                    hi, lo = split(perts[k])
                    right = jnp.concatenate([hi, hi, lo] + zero_rows(wide - 3 * members), axis=0)
                    projs.append(jnp.dot(left[batch, 0:taken], right, preferred_element_type=jnp.float32))
                for k in range(len(xs)):
                    w_hi, w_lo = split(projs[k] * locs[k // fields][batch])
                    if taken == third:
                        stack = jnp.concatenate([w_hi, w_hi, w_lo] + zero_rows(2 * tcols - 3 * third), axis=0)
                        change = jnp.dot(back3[batch], stack, preferred_element_type=jnp.float32)
                    elif taken == tcols:
                        stack = jnp.concatenate([w_hi, w_lo], axis=0)
                        one = jnp.dot(back2[batch], stack, preferred_element_type=jnp.float32)
                        change = one[:tall] + one[tall:]
                    else:
                        one = jnp.dot(back[batch], w_hi, preferred_element_type=jnp.float32)
                        two = jnp.dot(back[batch, 0:tall], w_lo, preferred_element_type=jnp.float32)
                        change = one[:tall] + one[tall:] + two
                    perts[k] = perts[k] + change[:members]
                    means[k] = means[k] + change[members : members + 1]
            for k in range(len(xs)):
                x = means[k] + perts[k]
                for d in range(2):
                    start = (k % fields) * members * high + 2 * (together * q + k // fields) + d
                    lines[pl.ds(start, members, stride=high), :] = x[:, d * tcols : (d + 1) * tcols]
            return carry

        together = high // 2 if taken == third else 1
        lax.fori_loop(0, high // (2 * together), pairs, 0)

    most = jnp.maximum(active_ref[0], active_ref[1])

    @pl.when(most <= third)
    def _():
        run(third)

    @pl.when((most > third) & (most <= tcols))
    def _():
        run(tcols)

    @pl.when(most > tcols)
    def _():
        run(depth)


def on_device(n_lat, n_lon, ensemble, courant_cols, courant_rows, obs_value, obs_error, obs_cell, obs_kind, obs_live, obs_list):
    fields, members, trows, tcols = ensemble.shape
    slots = obs_value.shape[1]
    f32, i32 = jnp.float32, jnp.int32
    vmem = pl.BlockSpec(memory_space=pltpu.VMEM)
    smem = pl.BlockSpec(memory_space=pltpu.SMEM)
    lines = ensemble.reshape(fields * members * trows, tcols)
    raw = (lines, courant_cols, courant_rows, obs_value, obs_error, obs_live, obs_cell, jnp.transpose(obs_list, (2, 0, 1)))
    state, sides, tables = pl.pallas_call(
        functools.partial(exchange_kernel, (fields, members, trows, tcols, slots, n_lat, n_lon)),
        out_shape=(
            jax.ShapeDtypeStruct((fields * trows, members, tcols), f32),
            jax.ShapeDtypeStruct((2, members, tcols), f32),
            jax.ShapeDtypeStruct((2, 9, slots, tcols), f32),
        ),
        in_specs=[pl.BlockSpec(memory_space=pltpu.HBM)] * len(raw) + [smem, smem],
        out_specs=(pl.BlockSpec(memory_space=pltpu.HBM), vmem, vmem),
        scratch_shapes=[pltpu.VMEM((fields * trows, members, tcols), f32)] + [pltpu.VMEM(part.shape, part.dtype) for part in raw] + [
            pltpu.VMEM((2, EXTRA, tcols), f32),
            pltpu.VMEM((fields, trows + 2, members, tcols), f32),
            pltpu.VMEM((2, members, tcols), f32),
            pltpu.VMEM((2, members, tcols), f32),
            pltpu.VMEM((2, 9, slots, tcols), f32),
            pltpu.SemaphoreType.DMA((len(raw) - 1 + fields,)),
        ] + [pltpu.SemaphoreType.DMA((2,))] * 4 + [pltpu.SemaphoreType.DMA((2, 9))] * 2 + [pltpu.SemaphoreType.DMA],
        compiler_params=pltpu.CompilerParams(
            collective_id=0, has_side_effects=True, vmem_limit_bytes=64 * 2**20),
        name="exchange",
    )(*raw, obs_cell, obs_kind)

    high = 8
    depth = -(-9 * slots // 16) * 16
    tall = -(-(members + 1) // 16) * 16
    wide = -(-3 * members // tcols) * tcols
    return pl.pallas_call(
        functools.partial(update_kernel, (fields, members, trows, tcols, slots, high)),
        grid=(trows // high,),
        out_shape=jax.ShapeDtypeStruct(ensemble.shape, f32),
        in_specs=[
            pl.BlockSpec((fields, high, members, tcols), lambda i: (0, i, 0, 0)),
            pl.BlockSpec((2, members, tcols), lambda i: (0, 0, 0)),
            pl.BlockSpec((2, 9, slots, tcols), lambda i: (0, 0, 0, 0)),
        ],
        out_specs=pl.BlockSpec((fields, members, high, tcols), lambda i: (0, 0, i, 0)),
        scratch_shapes=[
            pltpu.VMEM((2, depth, wide), jnp.bfloat16),
            pltpu.VMEM((2, 2 * tall, depth), jnp.bfloat16),
            pltpu.VMEM((2, tall, 2 * tcols), jnp.bfloat16),
            pltpu.VMEM((2, 2 * tall, 2 * tcols), jnp.bfloat16),
            pltpu.VMEM((2, depth, tcols), f32),
            pltpu.VMEM((2, depth, tcols), f32),
            pltpu.SMEM((2,), i32),
        ],
        compiler_params=pltpu.CompilerParams(vmem_limit_bytes=64 * 2**20),
        name="update",
    )(state.reshape(fields, trows, members, tcols), sides, tables)


def solution(mesh):
    placed = (
        P(None, None, "lat", "lon"),
        P(None, "lat", "lon"),
        P(None, "lat", "lon"),
        P(None, ("lat", "lon")),
        P(None, ("lat", "lon")),
        P(None, ("lat", "lon")),
        P(None, ("lat", "lon")),
        P(None, ("lat", "lon")),
        P(None, ("lat", "lon"), None),
    )
    return jax.shard_map(
        functools.partial(on_device, mesh.shape["lat"], mesh.shape["lon"]),
        mesh=mesh,
        in_specs=placed,
        out_specs=P(None, None, "lat", "lon"),
        check_vma=False,
    )
```
